32 devices in a mesh: row: 8 (over y, x, core), col: 4 (over z).
Axes of the slice: x: 2, y: 2, z: 4, core: 2. Of those that a mesh axis runs over, the one named last changes fastest.
Arguments:
- cotangent: bfloat16 [12288, 256], P(('row', 'col')), may hold values from -6 to 6
- seed_label: int32 [12288], P(('row', 'col')), may hold values from 0 to 511
- tile_values: bfloat16 [8, 4, 8, 48, 128, 128], P('row', 'col'), may hold values from 0 to 0.008239746
- tile_rows: int32 [8, 4, 8, 48], P('row', 'col'), may hold values from 0 to 11
- tile_cols: int32 [8, 4, 8, 48], P('row', 'col'), may hold values from 0 to 2
- tile_scale: int32 [8, 4, 8, 48], P('row', 'col'), may hold values from 0 to 4
Outputs:
- first_grad: bfloat16 [12288, 256], P(('row', 'col'))
- label_grad: bfloat16 [12288, 256], P(('row', 'col'))
The draws below stay inside these ranges and needn't reach their ends.
All inputs are finite; a program needn't handle non-finite values.
Results may differ from the reference program's by a relative error of at most 0.019.
Values may be sent and summed in bfloat16 or wider, within the bound.
No kernel may reach another device: no remote copies, remote signals or barrier semaphores. Data moves between devices by JAX's collectives and lax.ppermute only.
A program may use at most 64 MiB of HBM per device.

```python
import jax
import jax.numpy as jnp
from jax import lax

CLS = 256
TILE = 128
SEG = 384
TPR = 48
BPS = 3
NODES = 12288
N_ROW = 8
N_COL = 4


def touch_ends(array, key, smallest, top_value):
    longest = array.shape.index(max(array.shape))
    spots = []
    for shift in (0, 1):
        where = [jax.random.randint(jax.random.fold_in(key, axis), (), 0, length) for axis, length in enumerate(array.shape)]
        where[longest] = (where[longest] + shift) % array.shape[longest]
        spots.append(tuple(where))
    return array.at[spots[0]].set(smallest).at[spots[1]].set(top_value)


def level_of(rng, shape, pieces, low, top_value):
    gain, own = 1.0, jax.random.fold_in(rng, 6)
    for dim, shards_of in pieces:
        heights = jnp.exp(jax.random.uniform(jax.random.fold_in(own, dim), (shards_of,), jnp.float32, low / len(pieces), top_value / len(pieces)))
        gain = gain * jnp.repeat(heights, shape[dim] // shards_of).reshape([-1 if axis == dim else 1 for axis in range(len(shape))])
    return gain


def noise(stream_key, extent, deviation, most, shards=(), kind=jnp.bfloat16):
    drawn = jax.random.normal(stream_key, extent, jnp.float32) * deviation
    if len(shards) > 0:
        drawn = level_of(stream_key, extent, shards, -0.22, 0.18) * drawn
    return jnp.clip(drawn, min=-most, max=most).astype(kind)


def setup_inputs(seed: int = 0) -> dict:
    streams_of = jax.random.split(jax.random.key(seed), 7)
    cotangent = noise(streams_of[0], (NODES, CLS), 1.0, 6.0, ((0, 32),))
    seed_label = touch_ends(jax.random.randint(streams_of[1], (NODES,), 0, 2 * CLS), jax.random.fold_in(streams_of[1], 1), 0, (2 * CLS) - 1).astype(jnp.int32)
    tile_values = jnp.clip(0.008239746 * jax.random.uniform(streams_of[2], (N_ROW, N_COL, N_ROW, TPR, TILE, TILE), jnp.float32) ** level_of(streams_of[2], (N_ROW, N_COL, N_ROW, TPR, TILE, TILE), ((0, 8), (1, 4)), -0.2, 0.2), 0.0, 0.008239746).astype(jnp.bfloat16)
    tile_rows = touch_ends(jax.random.randint(streams_of[3], (N_ROW, N_COL, N_ROW, TPR), 0, N_COL * BPS), jax.random.fold_in(streams_of[3], 1), 0, (N_COL * BPS) - 1).astype(jnp.int32)
    tile_cols = touch_ends(jax.random.randint(streams_of[4], (N_ROW, N_COL, N_ROW, TPR), 0, BPS), jax.random.fold_in(streams_of[4], 1), 0, BPS - 1).astype(jnp.int32)
    tile_scale = touch_ends(jax.random.randint(streams_of[5], (N_ROW, N_COL, N_ROW, TPR), 0, 5), jax.random.fold_in(streams_of[5], 1), 0, 4).astype(jnp.int32)
    return dict(cotangent=cotangent, seed_label=seed_label, tile_values=tile_values, tile_rows=tile_rows, tile_cols=tile_cols, tile_scale=tile_scale)


ALPHA = 0.9


def group_term(sources, tile_block, row_ids, col_ids, scale_ids):
    blocks = SEG // TILE
    picked = jnp.take(sources, row_ids, axis=0)
    products = jnp.einsum("tij,tic->tjc", tile_block.astype(jnp.float32), picked.astype(jnp.float32), precision=lax.Precision.HIGHEST)
    weights = scale_ids.astype(jnp.float32)[:, None] * (col_ids[:, None] == jnp.arange(blocks, dtype=jnp.int32)[None, :]).astype(jnp.float32)
    summed = jnp.einsum("tb,tjc->bjc", weights, products, precision=lax.Precision.HIGHEST)
    return summed.reshape(SEG, CLS)


def propagate(labels, tile_values, tile_rows, tile_cols, tile_scale):
    accum = jnp.zeros((N_ROW, N_COL, SEG, CLS), jnp.float32)

    def visit(device, accum):
        device = jnp.asarray(device).astype(jnp.int32)
        row_pos = device // N_COL
        col_pos = device % N_COL
        begin = (row_pos * (N_COL * SEG)).astype(jnp.int32)
        sources = lax.dynamic_slice_in_dim(labels, begin, N_COL * SEG, 0).reshape(N_COL * SEG // TILE, TILE, CLS)
        tile_item = (tile_values[row_pos, col_pos], tile_rows[row_pos, col_pos], tile_cols[row_pos, col_pos], tile_scale[row_pos, col_pos])
        group_sums = lax.map(lambda member: group_term(sources, member[0], member[1], member[2], member[3]), tile_item)
        rounded = lax.optimization_barrier(group_sums.astype(jnp.bfloat16)).astype(jnp.float32)
        zero = jnp.zeros((), jnp.int32)
        current = lax.dynamic_slice(accum, (zero, col_pos, zero, zero), (N_ROW, 1, SEG, CLS))
        return lax.dynamic_update_slice(accum, current + rounded[:, None], (zero, col_pos, zero, zero))

    accum = lax.fori_loop(0, N_ROW * N_COL, visit, accum)
    return accum.reshape(NODES, CLS)


def reference(cotangent, seed_label, tile_values, tile_rows, tile_cols, tile_scale):
    keep_mask = (seed_label[:, None] != jnp.arange(CLS, dtype=jnp.int32)[None, :]).astype(jnp.float32)
    first_in = (cotangent.astype(jnp.float32) * keep_mask).astype(jnp.bfloat16)
    first_grad = (ALPHA * propagate(first_in, tile_values, tile_rows, tile_cols, tile_scale)).astype(jnp.bfloat16)
    second_in = (first_grad.astype(jnp.float32) * keep_mask).astype(jnp.bfloat16)
    second = propagate(second_in, tile_values, tile_rows, tile_cols, tile_scale)
    label_grad = ALPHA * second + (1.0 - ALPHA) * keep_mask * (cotangent.astype(jnp.float32) + first_grad.astype(jnp.float32))
    return first_grad, label_grad.astype(jnp.bfloat16)
```

```python
import functools

import jax
import jax.numpy as jnp
from jax import lax
from jax.experimental import pallas as pl
from jax.experimental.pallas import tpu as pltpu
from jax.sharding import PartitionSpec as P

ALPHA = 0.9
CHUNKS = 2
VMEM_LIMIT = 40 * 1024 * 1024


def params(limit=VMEM_LIMIT):
    return pltpu.CompilerParams(vmem_limit_bytes=limit)


def keep_of(seed_row, first_class, classes):
    ids = lax.broadcasted_iota(jnp.int32, (classes, seed_row.shape[1]), 0) + first_class
    return ids != seed_row


def prepare_kernel(cot_ref, seed_ref, *out_refs):
    rows = out_refs[0].shape[0]
    for i, out_ref in enumerate(out_refs):
        part = cot_ref[:, i * rows : (i + 1) * rows].astype(jnp.float32).T
        keep = keep_of(seed_ref[...], i * rows, rows)
        out_ref[...] = jnp.where(keep, part, 0.0).astype(out_ref.dtype)


def prepare(cotangent, seed_row):
    segment, classes = cotangent.shape
    shape = jax.ShapeDtypeStruct((classes // CHUNKS, segment), jnp.bfloat16)
    return pl.pallas_call(
        prepare_kernel,
        out_shape=[shape] * CHUNKS,
        name="prepare",
        compiler_params=params(),
    )(cotangent, seed_row)


def densify_kernel(place_ref, rows_ref, cols_ref, scale_ref, tiles_ref, out_ref, total_ref):
    slots, tile = tiles_ref.shape[3], tiles_ref.shape[4]
    blocks = out_ref.shape[2] // tile
    target = jnp.bitwise_xor(place_ref[0], pl.program_id(0))
    mine = place_ref[1]
    total_ref[...] = jnp.zeros_like(total_ref)

    def add(slot, carry):
        row, col = rows_ref[target, slot], cols_ref[target, slot]
        owner = row // blocks
        place = jnp.bitwise_xor(owner, mine) * blocks + row - owner * blocks
        scale = scale_ref[target, slot].astype(jnp.float32)
        where = (
            pl.ds(pl.multiple_of(place * tile, tile), tile),
            pl.ds(pl.multiple_of(col * tile, tile), tile),
        )
        total_ref[where] += scale * tiles_ref[0, 0, 0, slot].astype(jnp.float32)
        return carry

    lax.fori_loop(0, slots, add, 0)
    out_ref[0] = total_ref[...].astype(out_ref.dtype)


def densify(place, tile_values, tile_rows, tile_cols, tile_scale, depth, segment):
    _, _, targets, slots, tile, _ = tile_values.shape
    return pl.pallas_call(
        densify_kernel,
        grid_spec=pltpu.PrefetchScalarGridSpec(
            num_scalar_prefetch=4,
            grid=(targets,),
            in_specs=[
                pl.BlockSpec(
                    (1, 1, 1, slots, tile, tile),
                    lambda m, place, *_: (0, 0, jnp.bitwise_xor(place[0], m), 0, 0, 0),
                )
            ],
            out_specs=pl.BlockSpec((1, depth, segment), lambda m, *_: (m, 0, 0)),
            scratch_shapes=[pltpu.VMEM((depth, segment), jnp.float32)],
        ),
        out_shape=jax.ShapeDtypeStruct((targets, depth, segment), jnp.bfloat16),
        name="densify",
        compiler_params=params(),
    )(place, tile_rows[0, 0], tile_cols[0, 0], tile_scale[0, 0], tile_values)


def multiply_kernel(parts, *refs):
    label_refs, matrix_ref, out_ref = refs[:parts], refs[parts], refs[parts + 1]
    segment = matrix_ref.shape[2]
    total = None
    for i, label_ref in enumerate(label_refs):
        term = jnp.dot(
            label_ref[...],
            matrix_ref[0, i * segment : (i + 1) * segment, :],
            preferred_element_type=jnp.float32,
        )
        total = term if total is None else total + term
    out_ref[0] = total.astype(out_ref.dtype)


def multiply(labels, matrix, odd, dtype):
    targets, depth, segment = matrix.shape
    rows = labels[0].shape[0]
    return pl.pallas_call(
        functools.partial(multiply_kernel, len(labels)),
        grid=(targets // 2,),
        in_specs=[pl.BlockSpec((rows, segment), lambda m: (0, 0))] * len(labels)
        + [pl.BlockSpec((1, depth, segment), lambda m: (2 * m + odd, 0, 0))],
        out_specs=pl.BlockSpec((1, rows, segment), lambda m: (m, 0, 0)),
        out_shape=jax.ShapeDtypeStruct((targets // 2, rows, segment), dtype),
        name="multiply_theirs" if odd else "multiply_mine",
        compiler_params=params(),
        cost_estimate=pl.CostEstimate(
            flops=targets * depth * segment * rows,
            bytes_accessed=targets * depth * segment,
            transcendentals=0,
        ),
    )(*labels, matrix)


def pair_kernel(mine_ref, theirs_ref, *out_refs):
    for i, out_ref in enumerate(out_refs):
        total = mine_ref[i] + theirs_ref[i].astype(jnp.float32)
        out_ref[...] = total.astype(out_ref.dtype)


def pair(mine, theirs):
    count, rows, segment = mine.shape
    return pl.pallas_call(
        pair_kernel,
        out_shape=[jax.ShapeDtypeStruct((rows, segment), jnp.float32)]
        + [jax.ShapeDtypeStruct((rows, segment), jnp.bfloat16)] * (count - 1),
        name="pair_sum",
        compiler_params=params(),
    )(mine, theirs)


def middle_kernel(first_class, seed_ref, *refs):
    pieces, (grad_ref, next_ref) = refs[:-2], refs[-2:]
    total = pieces[0][...]
    for piece in pieces[1:]:
        total = total + piece[...].astype(jnp.float32)
    grad = (ALPHA * total).astype(jnp.bfloat16)
    grad_ref[...] = grad.astype(jnp.float32).T.astype(jnp.bfloat16)
    keep = keep_of(seed_ref[...], first_class, grad.shape[0])
    next_ref[...] = jnp.where(keep, grad.astype(jnp.float32), 0.0).astype(jnp.bfloat16)


def middle(seed_row, pieces, first_class):
    rows, segment = pieces[0].shape
    return pl.pallas_call(
        functools.partial(middle_kernel, first_class),
        out_shape=[
            jax.ShapeDtypeStruct((segment, rows), jnp.bfloat16),
            jax.ShapeDtypeStruct((rows, segment), jnp.bfloat16),
        ],
        name="first_grad",
        compiler_params=params(),
    )(seed_row, *pieces)


def final_kernel(first_ref, second_ref, *refs):
    pieces, out_ref = refs[:-1], refs[-1]
    total = pieces[0][...]
    for piece in pieces[1:]:
        total = total + piece[...].astype(jnp.float32)
    kept = first_ref[...].astype(jnp.float32) + second_ref[...].astype(jnp.float32)
    out_ref[...] = (ALPHA * total + (1.0 - ALPHA) * kept).T.astype(jnp.bfloat16)


def final(first_in, second_in, pieces):
    rows, segment = first_in.shape
    return pl.pallas_call(
        final_kernel,
        out_shape=jax.ShapeDtypeStruct((segment, rows), jnp.bfloat16),
        name="label_grad",
        compiler_params=params(),
    )(first_in, second_in, *pieces)


def flip(array, axis, size, bits):
    return lax.ppermute(array, axis, [(i, i ^ bits) for i in range(size)])


def gather(labels, n_col):
    return [labels] + [flip(labels, "col", n_col, k) for k in range(1, n_col)]


def reduce(labels, matrix, n_row):
    theirs = multiply(labels, matrix, 1, jnp.bfloat16)
    arrived = flip(theirs, "row", n_row, 1)
    mine = multiply(labels, matrix, 0, jnp.float32)
    own, *others = pair(mine, arrived)
    return [own] + [flip(part, "row", n_row, 2 * (j + 1)) for j, part in enumerate(others)]


def local(n_row, n_col, cotangent, seed_label, tile_values, tile_rows, tile_cols, tile_scale):
    segment, classes = cotangent.shape
    rows = classes // CHUNKS
    place = jnp.stack([lax.axis_index("row"), lax.axis_index("col")]).astype(jnp.int32)
    seed_row = seed_label[None, :]
    first_in = prepare(cotangent, seed_row)
    matrix = densify(
        place, tile_values, tile_rows, tile_cols, tile_scale, n_col * segment, segment
    )
    grads, seconds = [], []
    for i in range(CHUNKS):
        pieces = reduce(gather(first_in[i], n_col), matrix, n_row)
        grad, second_in = middle(seed_row, pieces, i * rows)
        grads.append(grad)
        seconds.append(second_in)
    results = []
    for i in range(CHUNKS):
        pieces = reduce(gather(seconds[i], n_col), matrix, n_row)
        results.append(final(first_in[i], seconds[i], pieces))
    return jnp.concatenate(grads, axis=1), jnp.concatenate(results, axis=1)


def solution(mesh):
    return jax.shard_map(
        functools.partial(local, mesh.shape["row"], mesh.shape["col"]),
        mesh=mesh,
        in_specs=(
            P(("row", "col"), None),
            P(("row", "col")),
            P("row", "col", None, None, None, None),
            P("row", "col", None, None),
            P("row", "col", None, None),
            P("row", "col", None, None),
        ),
        out_specs=(P(("row", "col"), None), P(("row", "col"), None)),
        check_vma=False,
    )
```

```python
import functools

import jax
import jax.numpy as jnp
from jax import lax
from jax.experimental import pallas as pl
from jax.experimental.pallas import tpu as pltpu
from jax.sharding import PartitionSpec as P

ALPHA = 0.9
CHUNKS = 2
VMEM_LIMIT = 40 * 1024 * 1024
CHEAP = pl.CostEstimate(flops=1, bytes_accessed=1, transcendentals=0)


def params():
    return pltpu.CompilerParams(vmem_limit_bytes=VMEM_LIMIT)


def after(arrays, *others):
    return lax.optimization_barrier((arrays, others))[0]


def keep_of(seed_row, first_class, classes):
    ids = lax.broadcasted_iota(jnp.int32, (classes, seed_row.shape[1]), 0) + first_class
    return ids != seed_row


def prepare_kernel(cot_ref, seed_ref, out_ref, cot, seed, semaphores):
    copies = [
        pltpu.make_async_copy(cot_ref, cot, semaphores.at[0]),
        pltpu.make_async_copy(seed_ref, seed, semaphores.at[1]),
    ]
    for copy in copies:
        copy.start()
    for copy in copies:
        copy.wait()
    part = cot[...].astype(jnp.float32).T
    keep = keep_of(seed[...][None, :], 0, part.shape[0])
    out_ref[...] = jnp.where(keep, part, 0.0).astype(out_ref.dtype)


def prepare(cotangent, seed_label):
    segment, classes = cotangent.shape
    cotangent, seed_label = (
        pltpu.with_memory_space_constraint(array, pltpu.HBM) for array in (cotangent, seed_label)
    )
    return pl.pallas_call(
        prepare_kernel,
        in_specs=[pl.BlockSpec(memory_space=pltpu.HBM)] * 2,
        out_shape=jax.ShapeDtypeStruct((classes, segment), jnp.bfloat16),
        scratch_shapes=[
            pltpu.VMEM(cotangent.shape, cotangent.dtype),
            pltpu.VMEM(seed_label.shape, seed_label.dtype),
            pltpu.SemaphoreType.DMA((2,)),
        ],
        name="prepare",
        compiler_params=params(),
        cost_estimate=CHEAP,
    )(cotangent, seed_label)


def slot_codes(col_place, blocks, tile_rows, tile_cols, tile_scale):
    slots = tile_rows.shape[1]
    ids = jnp.arange(slots, dtype=jnp.int32)
    place = ((tile_rows // blocks) ^ col_place) * blocks + tile_rows % blocks
    codes = (((place << 4) | tile_cols) << 16) | (ids[None, :] << 8) | tile_scale
    position = jnp.sum((codes[:, None, :] < codes[:, :, None]).astype(jnp.int32), axis=-1)
    return jnp.sum(jnp.where(position[:, :, None] == ids, codes[:, :, None], 0), axis=1)


def densify_kernel(odd, place_ref, codes_ref, tiles_ref, out_ref):
    slots, tile = tiles_ref.shape[3], tiles_ref.shape[4]
    depth, segment = out_ref.shape[0], out_ref.shape[1] // pl.num_programs(0)
    step = pl.program_id(0)
    target = jnp.bitwise_xor(place_ref[0], 2 * step + odd)
    base = step * segment
    out_ref[:, pl.ds(pl.multiple_of(base, tile), segment)] = jnp.zeros(
        (depth, segment), out_ref.dtype
    )

    def add(position, carry):
        total, before = carry
        code = codes_ref[target, position]
        block, slot, scale = code >> 16, (code >> 8) & 255, code & 255
        term = tiles_ref[0, 0, 0, slot].astype(jnp.float32) * scale.astype(jnp.float32)
        total = total * (block == before).astype(jnp.float32) + term
        row, col = (block >> 4) * tile, base + (block & 15) * tile
        out_ref[
            pl.ds(pl.multiple_of(row, tile), tile), pl.ds(pl.multiple_of(col, tile), tile)
        ] = total.astype(out_ref.dtype)
        return total, block

    start = (jnp.zeros((tile, tile), jnp.float32), jnp.int32(-1))
    lax.fori_loop(0, slots, add, start, unroll=4)


def densify(place, codes, tile_values, odd, depth, segment):
    _, _, targets, slots, tile, _ = tile_values.shape
    half = targets // 2
    return pl.pallas_call(
        functools.partial(densify_kernel, odd),
        grid_spec=pltpu.PrefetchScalarGridSpec(
            num_scalar_prefetch=2,
            grid=(half,),
            in_specs=[
                pl.BlockSpec(
                    (1, 1, 1, slots, tile, tile),
                    lambda m, place, _: (0, 0, jnp.bitwise_xor(place[0], 2 * m + odd), 0, 0, 0),
                )
            ],
            out_specs=pl.BlockSpec(memory_space=pltpu.VMEM),
        ),
        out_shape=jax.ShapeDtypeStruct((depth, half * segment), jnp.bfloat16),
        name="densify_theirs" if odd else "densify_mine",
        compiler_params=params(),
        cost_estimate=CHEAP,
    )(place, codes, tile_values)


def multiply_kernel(groups, first, rows, start, *refs):
    label_refs, matrix_ref, out_ref = refs[:-2], refs[-2], refs[-1]
    half, _, segment = out_ref.shape
    each = len(label_refs) // groups
    labels = jnp.concatenate(
        [
            jnp.concatenate(
                [ref[first : first + rows, :] for ref in label_refs[i * each : (i + 1) * each]],
                axis=1,
            )
            for i in range(groups)
        ],
        axis=0,
    )
    for i in range(0, half, 2):
        part = jnp.dot(
            labels,
            matrix_ref[:, (start + i) * segment : (start + i + 2) * segment],
            preferred_element_type=jnp.float32,
        )
        out_ref[i] = part[:, :segment].astype(out_ref.dtype)
        out_ref[i + 1] = part[:, segment:].astype(out_ref.dtype)


def multiply(groups, first, rows, matrix, dtype, name, start=0, count=None, weight=0):
    segment = groups[0][0].shape[1]
    depth, width = matrix.shape
    count = width // segment if count is None else count
    total = len(groups) * rows
    return pl.pallas_call(
        functools.partial(multiply_kernel, len(groups), first, rows, start),
        out_shape=jax.ShapeDtypeStruct((count, total, segment), dtype),
        name=name,
        compiler_params=params(),
        cost_estimate=pl.CostEstimate(
            flops=2 * weight * depth * width * rows, bytes_accessed=1, transcendentals=0
        ),
    )(*[label for group in groups for label in group], matrix)


def pair_kernel(mine_ref, *refs):
    count = mine_ref.shape[0]
    theirs_refs, out_refs = refs[:-count], refs[-count:]
    theirs = [ref.at[i] for ref in theirs_refs for i in range(ref.shape[0])]
    for i, out_ref in enumerate(out_refs):
        total = mine_ref[i] + theirs[i][...].astype(jnp.float32)
        out_ref[...] = total.astype(out_ref.dtype)


def pair(mine, theirs):
    count, rows, segment = mine.shape
    return pl.pallas_call(
        pair_kernel,
        out_shape=[jax.ShapeDtypeStruct((rows, segment), jnp.float32)]
        + [jax.ShapeDtypeStruct((rows, segment), jnp.bfloat16)] * (count - 1),
        name="pair_sum",
        compiler_params=params(),
        cost_estimate=CHEAP,
    )(mine, *theirs)


def add_pieces(pieces):
    total = pieces[0][...]
    for piece in pieces[1:]:
        total = total + piece[...].astype(jnp.float32)
    return total


def middle_kernel(first_class, seed_ref, *refs):
    pieces, (grad_ref, next_ref) = refs[:-2], refs[-2:]
    grad = (ALPHA * add_pieces(pieces)).astype(jnp.bfloat16)
    grad_ref[...] = grad
    keep = keep_of(seed_ref[...][None, :], first_class, grad.shape[0])
    next_ref[...] = jnp.where(keep, grad.astype(jnp.float32), 0.0).astype(jnp.bfloat16)


def middle(seed_label, pieces, first_class):
    shape = jax.ShapeDtypeStruct(pieces[0].shape, jnp.bfloat16)
    return pl.pallas_call(
        functools.partial(middle_kernel, first_class),
        out_shape=[shape, shape],
        name="first_grad",
        compiler_params=params(),
        cost_estimate=CHEAP,
    )(seed_label, *pieces)


def transposed_kernel(*refs):
    part_refs, out_ref = refs[:-1], refs[-1]
    rows = part_refs[0].shape[0]
    for i, ref in enumerate(part_refs):
        part = ref[...].astype(jnp.float32).T.astype(out_ref.dtype)
        out_ref[:, i * rows : (i + 1) * rows] = part


def transposed(parts):
    rows, segment = parts[0].shape
    return pl.pallas_call(
        transposed_kernel,
        out_shape=jax.ShapeDtypeStruct((segment, len(parts) * rows), jnp.bfloat16),
        name="first_grad_out",
        compiler_params=params(),
        cost_estimate=CHEAP,
    )(*parts)


def label_part(first, first_ref, second_ref, pieces):
    rows = second_ref.shape[0]
    kept = first_ref[first : first + rows, :].astype(jnp.float32)
    kept = kept + second_ref[...].astype(jnp.float32)
    return (ALPHA * add_pieces(pieces) + (1.0 - ALPHA) * kept).T.astype(jnp.bfloat16)


def label_kernel(first, first_ref, second_ref, *refs):
    refs[-1][...] = label_part(first, first_ref, second_ref, refs[:-1])


def label(first_in, second_in, pieces, first):
    rows, segment = second_in.shape
    return pl.pallas_call(
        functools.partial(label_kernel, first),
        out_shape=jax.ShapeDtypeStruct((segment, rows), jnp.bfloat16),
        name="label_grad",
        compiler_params=params(),
        cost_estimate=CHEAP,
    )(first_in, second_in, *pieces)


def last_label_kernel(first, count, first_ref, second_ref, *refs):
    ready, pieces, out_ref = refs[:count], refs[count:-1], refs[-1]
    rows = second_ref.shape[0]
    for i, ref in enumerate(ready):
        out_ref[:, i * rows : (i + 1) * rows] = ref[...]
    out_ref[:, first : first + rows] = label_part(first, first_ref, second_ref, pieces)


def last_label(first_in, second_in, pieces, first, ready):
    classes, segment = first_in.shape
    return pl.pallas_call(
        functools.partial(last_label_kernel, first, len(ready)),
        out_shape=jax.ShapeDtypeStruct((segment, classes), jnp.bfloat16),
        name="label_grad_out",
        compiler_params=params(),
        cost_estimate=CHEAP,
    )(first_in, second_in, *ready, *pieces)


def flip(array, axis, size, bits):
    return lax.ppermute(array, axis, [(i, i ^ bits) for i in range(size)])


def gather(labels, n_col):
    others = {k: flip(labels, "col", n_col, k) for k in reversed(range(1, n_col))}
    return [labels] + [others[k] for k in range(1, n_col)]


def spread(own_and_others, n_row):
    own, *others = own_and_others
    return [own] + [flip(part, "row", n_row, 2 * (j + 1)) for j, part in enumerate(others)]


def local(n_row, n_col, cotangent, seed_label, tile_values, tile_rows, tile_cols, tile_scale):
    segment, classes = cotangent.shape
    rows, depth = classes // CHUNKS, n_col * segment
    blocks = segment // tile_values.shape[-1]
    firsts = [i * rows for i in range(CHUNKS)]
    col_place = lax.axis_index("col").astype(jnp.int32)
    place = jnp.stack([lax.axis_index("row").astype(jnp.int32), col_place])
    first_in = prepare(cotangent, seed_label)
    codes = slot_codes(col_place, blocks, tile_rows[0, 0], tile_cols[0, 0], tile_scale[0, 0])
    to_theirs = densify(place, codes, tile_values, 1, depth, segment)
    codes = after(codes, to_theirs)
    to_mine = densify(place, codes, tile_values, 0, depth, segment)

    arrived = after(gather(first_in, n_col), to_mine)
    theirs, mines, swapped, pieces = [], [], [], []
    done = to_mine
    for i, first in enumerate(firsts):
        labels = after(arrived, done)
        done = multiply([labels], first, rows, to_theirs, jnp.bfloat16, "multiply_theirs")
        swapped.append(flip(done, "row", n_row, 1))
        if i + 1 < CHUNKS:
            labels = after(arrived, done)
            done = multiply([labels], first, rows, to_mine, jnp.float32, "multiply_mine")
            mines.append(done)
    for i, first in enumerate(firsts):
        if i + 1 == CHUNKS:
            labels = after(arrived, done)
            done = multiply([labels], first, rows, to_mine, jnp.float32, "multiply_mine")
            mines.append(done)
        done = pair(after(mines[i], done), swapped[i : i + 1])
        pieces.append(spread(done, n_row))
    grads, seconds, sources = [], [], []
    for i, first in enumerate(firsts):
        grad, second_in = middle(seed_label, after(pieces[i], done), first)
        done = [grad, second_in]
        grads.append(grad)
        seconds.append(second_in)
        sources.append(gather(second_in, n_col))

    pieces = []
    for i in range(CHUNKS):
        labels = after(sources[i], done)
        theirs = multiply([labels], 0, rows, to_theirs, jnp.bfloat16, "multiply_theirs")
        swapped = flip(theirs, "row", n_row, 1)
        labels = after(sources[i], theirs)
        mine = multiply(
            [labels], 0, rows, to_mine, jnp.float32, "multiply_mine", weight=20
        )
        done = pair(mine, [swapped])
        pieces.append(spread(done, n_row))
    results = []
    for i in range(CHUNKS - 1):
        done = label(first_in, seconds[i], after(pieces[i], done), firsts[i])
        results.append(done)
    first_grad = transposed(after(grads, done))
    pieces = after(pieces[-1], first_grad)
    return first_grad, last_label(first_in, seconds[-1], pieces, firsts[-1], results)


def solution(mesh):
    return jax.shard_map(
        functools.partial(local, mesh.shape["row"], mesh.shape["col"]),
        mesh=mesh,
        in_specs=(
            P(("row", "col"), None),
            P(("row", "col")),
            P("row", "col", None, None, None, None),
            P("row", "col", None, None),
            P("row", "col", None, None),
            P("row", "col", None, None),
        ),
        out_specs=(P(("row", "col"), None), P(("row", "col"), None)),
        check_vma=False,
    )
```

```python
import functools

import jax
import jax.numpy as jnp
from jax import lax
from jax.experimental import pallas as pl
from jax.experimental.pallas import tpu as pltpu
from jax.sharding import PartitionSpec as P

ALPHA = 0.9
VMEM_LIMIT = 40 * 1024 * 1024
CHEAP = pl.CostEstimate(flops=1, bytes_accessed=1, transcendentals=0)


def params():
    return pltpu.CompilerParams(vmem_limit_bytes=VMEM_LIMIT)


def after(arrays, *others):
    return lax.optimization_barrier((arrays, others))[0]


def keep_of(seed_row, first_class, classes):
    ids = lax.broadcasted_iota(jnp.int32, (classes, seed_row.shape[1]), 0) + first_class
    return ids != seed_row


def prepare_kernel(cot_ref, seed_ref, out_ref, cot, seed, semaphores):
    copies = [
        pltpu.make_async_copy(cot_ref, cot, semaphores.at[0]),
        pltpu.make_async_copy(seed_ref, seed, semaphores.at[1]),
    ]
    for copy in copies:
        copy.start()
    for copy in copies:
        copy.wait()
    part = cot[...].astype(jnp.float32).T
    keep = keep_of(seed[...][None, :], 0, part.shape[0])
    out_ref[...] = jnp.where(keep, part, 0.0).astype(out_ref.dtype)


def prepare(cotangent, seed_label):
    segment, classes = cotangent.shape
    cotangent, seed_label = (
        pltpu.with_memory_space_constraint(array, pltpu.HBM) for array in (cotangent, seed_label)
    )
    return pl.pallas_call(
        prepare_kernel,
        in_specs=[pl.BlockSpec(memory_space=pltpu.HBM)] * 2,
        out_shape=jax.ShapeDtypeStruct((classes, segment), jnp.bfloat16),
        scratch_shapes=[
            pltpu.VMEM(cotangent.shape, cotangent.dtype),
            pltpu.VMEM(seed_label.shape, seed_label.dtype),
            pltpu.SemaphoreType.DMA((2,)),
        ],
        name="prepare",
        compiler_params=params(),
        cost_estimate=CHEAP,
    )(cotangent, seed_label)


def slot_codes(col_place, blocks, tile_rows, tile_cols, tile_scale):
    slots = tile_rows.shape[1]
    ids = jnp.arange(slots, dtype=jnp.int32)
    place = ((tile_rows // blocks) ^ col_place) * blocks + tile_rows % blocks
    codes = (((place << 4) | tile_cols) << 16) | (ids[None, :] << 8) | tile_scale
    position = jnp.sum((codes[:, None, :] < codes[:, :, None]).astype(jnp.int32), axis=-1)
    return jnp.sum(jnp.where(position[:, :, None] == ids, codes[:, :, None], 0), axis=1)


def densify_kernel(odd, place_ref, codes_ref, tiles_ref, out_ref):
    slots, tile = tiles_ref.shape[3], tiles_ref.shape[4]
    depth, segment = out_ref.shape[0], out_ref.shape[1] // pl.num_programs(0)
    step = pl.program_id(0)
    target = jnp.bitwise_xor(place_ref[0], 2 * step + odd)
    base = step * segment
    out_ref[:, pl.ds(pl.multiple_of(base, tile), segment)] = jnp.zeros(
        (depth, segment), out_ref.dtype
    )

    def add(position, carry):
        total, before = carry
        code = codes_ref[target, position]
        block, slot, scale = code >> 16, (code >> 8) & 255, code & 255
        term = tiles_ref[0, 0, 0, slot].astype(jnp.float32) * scale.astype(jnp.float32)
        total = total * (block == before).astype(jnp.float32) + term
        row, col = (block >> 4) * tile, base + (block & 15) * tile
        out_ref[
            pl.ds(pl.multiple_of(row, tile), tile), pl.ds(pl.multiple_of(col, tile), tile)
        ] = total.astype(out_ref.dtype)
        return total, block

    start = (jnp.zeros((tile, tile), jnp.float32), jnp.int32(-1))
    lax.fori_loop(0, slots, add, start, unroll=4)


def densify(place, codes, tile_values, odd, depth, segment):
    _, _, targets, slots, tile, _ = tile_values.shape
    half = targets // 2
    return pl.pallas_call(
        functools.partial(densify_kernel, odd),
        grid_spec=pltpu.PrefetchScalarGridSpec(
            num_scalar_prefetch=2,
            grid=(half,),
            in_specs=[
                pl.BlockSpec(
                    (1, 1, 1, slots, tile, tile),
                    lambda m, place, _: (0, 0, jnp.bitwise_xor(place[0], 2 * m + odd), 0, 0, 0),
                )
            ],
            out_specs=pl.BlockSpec(memory_space=pltpu.VMEM),
        ),
        out_shape=jax.ShapeDtypeStruct((depth, half * segment), jnp.bfloat16),
        name="densify_theirs" if odd else "densify_mine",
        compiler_params=params(),
        cost_estimate=CHEAP,
    )(place, codes, tile_values)


def multiply_kernel(groups, first, rows, start, *refs):
    label_refs, matrix_ref, out_ref = refs[:-2], refs[-2], refs[-1]
    half, _, segment = out_ref.shape
    each = len(label_refs) // groups
    labels = jnp.concatenate(
        [
            jnp.concatenate(
                [ref[first : first + rows, :] for ref in label_refs[i * each : (i + 1) * each]],
                axis=1,
            )
            for i in range(groups)
        ],
        axis=0,
    )
    for i in range(0, half, 2):
        part = jnp.dot(
            labels,
            matrix_ref[:, (start + i) * segment : (start + i + 2) * segment],
            preferred_element_type=jnp.float32,
        )
        out_ref[i] = part[:, :segment].astype(out_ref.dtype)
        out_ref[i + 1] = part[:, segment:].astype(out_ref.dtype)


def multiply(groups, first, rows, matrix, dtype, name, start=0, count=None, weight=0):
    segment = groups[0][0].shape[1]
    depth, width = matrix.shape
    count = width // segment if count is None else count
    total = len(groups) * rows
    return pl.pallas_call(
        functools.partial(multiply_kernel, len(groups), first, rows, start),
        out_shape=jax.ShapeDtypeStruct((count, total, segment), dtype),
        name=name,
        compiler_params=params(),
        cost_estimate=pl.CostEstimate(
            flops=2 * weight * depth * width * rows, bytes_accessed=1, transcendentals=0
        ),
    )(*[label for group in groups for label in group], matrix)


def pair_kernel(mine_ref, *refs):
    count = mine_ref.shape[0]
    theirs_refs, out_refs = refs[:-count], refs[-count:]
    theirs = [ref.at[i] for ref in theirs_refs for i in range(ref.shape[0])]
    for i, out_ref in enumerate(out_refs):
        total = mine_ref[i] + theirs[i][...].astype(jnp.float32)
        out_ref[...] = total.astype(out_ref.dtype)


def pair(mine, theirs):
    count, rows, segment = mine.shape
    return pl.pallas_call(
        pair_kernel,
        out_shape=[jax.ShapeDtypeStruct((rows, segment), jnp.float32)]
        + [jax.ShapeDtypeStruct((rows, segment), jnp.bfloat16)] * (count - 1),
        name="pair_sum",
        compiler_params=params(),
        cost_estimate=CHEAP,
    )(mine, *theirs)


def halve_kernel(kept_ref, arrived_ref, stay_ref, send_ref):
    for i in range(kept_ref.shape[0]):
        total = kept_ref[i] + arrived_ref[i].astype(jnp.float32)
        if i % 2:
            send_ref[i // 2] = total.astype(send_ref.dtype)
        else:
            stay_ref[i // 2] = total


def halve(kept, arrived):
    count, rows, segment = kept.shape
    shape = (count // 2, rows, segment)
    return pl.pallas_call(
        halve_kernel,
        out_shape=[
            jax.ShapeDtypeStruct(shape, jnp.float32),
            jax.ShapeDtypeStruct(shape, jnp.bfloat16),
        ],
        name="halve_sum",
        compiler_params=params(),
        cost_estimate=CHEAP,
    )(kept, arrived)


def add_pieces(pieces):
    total = pieces[0][...].reshape(pieces[0].shape[-2:])
    for piece in pieces[1:]:
        total = total + piece[...].reshape(total.shape).astype(jnp.float32)
    return total


def middle_kernel(first_class, seed_ref, *refs):
    pieces, (grad_ref, next_ref) = refs[:-2], refs[-2:]
    grad = (ALPHA * add_pieces(pieces)).astype(jnp.bfloat16)
    grad_ref[...] = grad
    keep = keep_of(seed_ref[...][None, :], first_class, grad.shape[0])
    next_ref[...] = jnp.where(keep, grad.astype(jnp.float32), 0.0).astype(jnp.bfloat16)


def middle(seed_label, pieces, first_class):
    shape = jax.ShapeDtypeStruct(pieces[0].shape[-2:], jnp.bfloat16)
    return pl.pallas_call(
        functools.partial(middle_kernel, first_class),
        out_shape=[shape, shape],
        name="first_grad",
        compiler_params=params(),
        cost_estimate=pl.CostEstimate(
            flops=10**10 if first_class == 0 else 1, bytes_accessed=1, transcendentals=0
        ),
    )(seed_label, *pieces)


def turn_kernel(part_ref, out_ref):
    out_ref[...] = part_ref[...].astype(jnp.float32).T.astype(out_ref.dtype)


def turn(part):
    rows, segment = part.shape
    return pl.pallas_call(
        turn_kernel,
        out_shape=jax.ShapeDtypeStruct((segment, rows), part.dtype),
        name="turn_grad",
        compiler_params=params(),
        cost_estimate=pl.CostEstimate(flops=10**10, bytes_accessed=1, transcendentals=0),
    )(part)


def first_out_kernel(*refs):
    ready, last_ref, out_ref = refs[:-2], refs[-2], refs[-1]
    rows = last_ref.shape[0]
    for i, ref in enumerate(ready):
        out_ref[:, i * rows : (i + 1) * rows] = ref[...]
    turned = last_ref[...].astype(jnp.float32).T.astype(out_ref.dtype)
    out_ref[:, len(ready) * rows :] = turned


def first_out(ready, last):
    rows, segment = last.shape
    return pl.pallas_call(
        first_out_kernel,
        out_shape=jax.ShapeDtypeStruct((segment, (len(ready) + 1) * rows), jnp.bfloat16),
        name="first_grad_out",
        compiler_params=params(),
        cost_estimate=CHEAP,
    )(*ready, last)


def label_part(first, first_ref, second_ref, pieces):
    rows = second_ref.shape[0]
    kept = first_ref[first : first + rows, :].astype(jnp.float32)
    kept = kept + second_ref[...].astype(jnp.float32)
    return (ALPHA * add_pieces(pieces) + (1.0 - ALPHA) * kept).T.astype(jnp.bfloat16)


def label_kernel(first, first_ref, second_ref, *refs):
    refs[-1][...] = label_part(first, first_ref, second_ref, refs[:-1])


def label(first_in, second_in, pieces, first):
    rows, segment = second_in.shape
    return pl.pallas_call(
        functools.partial(label_kernel, first),
        out_shape=jax.ShapeDtypeStruct((segment, rows), jnp.bfloat16),
        name="label_grad",
        compiler_params=params(),
        cost_estimate=CHEAP,
    )(first_in, second_in, *pieces)


def last_label_kernel(first, count, first_ref, second_ref, *refs):
    ready, pieces, out_ref = refs[:count], refs[count:-1], refs[-1]
    rows = second_ref.shape[0]
    for i, ref in enumerate(ready):
        out_ref[:, i * rows : (i + 1) * rows] = ref[...]
    out_ref[:, first : first + rows] = label_part(first, first_ref, second_ref, pieces)


def last_label(first_in, second_in, pieces, first, ready):
    classes, segment = first_in.shape
    return pl.pallas_call(
        functools.partial(last_label_kernel, first, len(ready)),
        out_shape=jax.ShapeDtypeStruct((segment, classes), jnp.bfloat16),
        name="label_grad_out",
        compiler_params=params(),
        cost_estimate=CHEAP,
    )(first_in, second_in, *ready, *pieces)


def flip(array, axis, size, bits):
    return lax.ppermute(array, axis, [(i, i ^ bits) for i in range(size)])


def gather(labels, n_col, late=(), waits=()):
    held = after(labels, waits) if late else labels
    return [labels] + [
        flip(held if k in late else labels, "col", n_col, k) for k in range(1, n_col)
    ]


def spread(parts, n_row, late=(), waits=()):
    own, *others = parts
    sent = []
    for j, part in enumerate(others, 1):
        part = after(part, waits) if j in late else part
        sent.append(flip(part, "row", n_row, 2 * j))
    return [own] + sent


def local(n_row, n_col, cotangent, seed_label, tile_values, tile_rows, tile_cols, tile_scale):
    segment, classes = cotangent.shape
    rows, depth = classes // 2, n_col * segment
    blocks, chips = segment // tile_values.shape[-1], n_row // 2
    col_place = lax.axis_index("col").astype(jnp.int32)
    place = jnp.stack([lax.axis_index("row").astype(jnp.int32), col_place])
    first_in = prepare(cotangent, seed_label)
    codes = slot_codes(col_place, blocks, tile_rows[0, 0], tile_cols[0, 0], tile_scale[0, 0])
    to_theirs = densify(place, codes, tile_values, 1, depth, segment)
    to_mine = densify(place, after(codes, to_theirs), tile_values, 0, depth, segment)

    def for_theirs(labels, first, waits):
        labels = after(labels, waits)
        part = multiply([labels], first, rows, to_theirs, jnp.bfloat16, "multiply_theirs")
        return part, flip(part, "row", n_row, 1)

    def for_mine(labels, first, waits, weight=0):
        labels = after(labels, waits)
        return multiply(
            [labels], first, rows, to_mine, jnp.float32, "multiply_mine", weight=weight
        )

    arrived = gather(first_in, n_col)
    theirs, swapped_a = for_theirs(arrived, 0, to_mine)
    mine = for_mine(arrived, 0, theirs)
    theirs, swapped_b = for_theirs(arrived, rows, mine)
    parts_a = pair(after(mine, theirs), [swapped_a])
    mine = for_mine(arrived, rows, parts_a, 20)
    pieces_a = spread(parts_a, n_row)
    done = halve(mine, swapped_b)
    pieces_b = [done[0], flip(done[1], "row", n_row, 2)]

    grad_a, second_a = middle(seed_label, after(pieces_a, done), 0)
    done, step = [grad_a, second_a], 4
    while step < n_row:
        done = halve(*after(pieces_b, done))
        pieces_b = [done[0], flip(done[1], "row", n_row, step)]
        step *= 2
    sources_a = gather(second_a, n_col, (1,), done)
    turned_a = turn(after(grad_a, done))
    grad_b, second_b = middle(seed_label, after(pieces_b, turned_a), rows)

    theirs, swapped_a = for_theirs(sources_a, 0, [grad_b, second_b])
    mine = for_mine(sources_a, 0, theirs, 20)
    sources_b = gather(second_b, n_col)
    parts_a = pair(mine, [swapped_a])
    theirs, swapped_b = for_theirs(sources_b, 0, parts_a)
    mine = for_mine(sources_b, 0, theirs, 20)
    pieces_a = spread(parts_a, n_row)
    parts_b = pair(mine, [swapped_b])
    pieces_b = spread(parts_b, n_row)

    label_a = label(first_in, second_a, after(pieces_a, parts_b), 0)
    first_grad = first_out([turned_a], after(grad_b, label_a))
    pieces_b = after(pieces_b, first_grad)
    return first_grad, last_label(first_in, second_b, pieces_b, rows, [label_a])


def solution(mesh):
    return jax.shard_map(
        functools.partial(local, mesh.shape["row"], mesh.shape["col"]),
        mesh=mesh,
        in_specs=(
            P(("row", "col"), None),
            P(("row", "col")),
            P("row", "col", None, None, None, None),
            P("row", "col", None, None),
            P("row", "col", None, None),
            P("row", "col", None, None),
        ),
        out_specs=(P(("row", "col"), None), P(("row", "col"), None)),
        check_vma=False,
    )
```

```python
import functools

import jax
import jax.numpy as jnp
from jax import lax
from jax.experimental import pallas as pl
from jax.experimental.pallas import tpu as pltpu
from jax.sharding import PartitionSpec as P

ALPHA = 0.9
VMEM_LIMIT = 40 * 1024 * 1024
CHEAP = pl.CostEstimate(flops=1, bytes_accessed=1, transcendentals=0)


def params():
    return pltpu.CompilerParams(vmem_limit_bytes=VMEM_LIMIT)


def after(arrays, *others):
    return lax.optimization_barrier((arrays, others))[0]


def keep_of(seed_row, first_class, classes):
    ids = lax.broadcasted_iota(jnp.int32, (classes, seed_row.shape[1]), 0) + first_class
    return ids != seed_row


def prepare_kernel(cot_ref, seed_ref, out_ref, cot, seed, semaphores):
    copies = [
        pltpu.make_async_copy(cot_ref, cot, semaphores.at[0]),
        pltpu.make_async_copy(seed_ref, seed, semaphores.at[1]),
    ]
    for copy in copies:
        copy.start()
    for copy in copies:
        copy.wait()
    part = cot[...].astype(jnp.float32).T
    keep = keep_of(seed[...][None, :], 0, part.shape[0])
    out_ref[...] = jnp.where(keep, part, 0.0).astype(out_ref.dtype)


def prepare(cotangent, seed_label):
    segment, classes = cotangent.shape
    cotangent, seed_label = (
        pltpu.with_memory_space_constraint(array, pltpu.HBM) for array in (cotangent, seed_label)
    )
    return pl.pallas_call(
        prepare_kernel,
        in_specs=[pl.BlockSpec(memory_space=pltpu.HBM)] * 2,
        out_shape=jax.ShapeDtypeStruct((classes, segment), jnp.bfloat16),
        scratch_shapes=[
            pltpu.VMEM(cotangent.shape, cotangent.dtype),
            pltpu.VMEM(seed_label.shape, seed_label.dtype),
            pltpu.SemaphoreType.DMA((2,)),
        ],
        name="prepare",
        compiler_params=params(),
        cost_estimate=CHEAP,
    )(cotangent, seed_label)


def slot_codes(col_place, blocks, tile_rows, tile_cols, tile_scale):
    slots = tile_rows.shape[1]
    ids = jnp.arange(slots, dtype=jnp.int32)
    place = ((tile_rows // blocks) ^ col_place) * blocks + tile_rows % blocks
    codes = (((place << 4) | tile_cols) << 16) | (ids[None, :] << 8) | tile_scale
    position = jnp.sum((codes[:, None, :] < codes[:, :, None]).astype(jnp.int32), axis=-1)
    return jnp.sum(jnp.where(position[:, :, None] == ids, codes[:, :, None], 0), axis=1)


def chip_offset(position, chips):
    return jnp.where(position == 0, 0, (position + chips - 3) % (chips - 1) + 1)


def densify_kernel(odd, place_ref, codes_ref, tiles_ref, out_ref):
    slots, tile = tiles_ref.shape[3], tiles_ref.shape[4]
    depth, segment = out_ref.shape[0], out_ref.shape[1] // pl.num_programs(0)
    step = pl.program_id(0)
    chip = chip_offset(step, pl.num_programs(0))
    target = jnp.bitwise_xor(place_ref[0], 2 * chip + odd)
    base = step * segment
    out_ref[:, pl.ds(pl.multiple_of(base, tile), segment)] = jnp.zeros(
        (depth, segment), out_ref.dtype
    )

    def add(position, carry):
        total, before = carry
        code = codes_ref[target, position]
        block, slot, scale = code >> 16, (code >> 8) & 255, code & 255
        term = tiles_ref[0, 0, 0, slot].astype(jnp.float32) * scale.astype(jnp.float32)
        total = total * (block == before).astype(jnp.float32) + term
        row, col = (block >> 4) * tile, base + (block & 15) * tile
        out_ref[
            pl.ds(pl.multiple_of(row, tile), tile), pl.ds(pl.multiple_of(col, tile), tile)
        ] = total.astype(out_ref.dtype)
        return total, block

    start = (jnp.zeros((tile, tile), jnp.float32), jnp.int32(-1))
    lax.fori_loop(0, slots, add, start, unroll=4)


def densify(place, codes, tile_values, odd, depth, segment):
    _, _, targets, slots, tile, _ = tile_values.shape
    half = targets // 2
    return pl.pallas_call(
        functools.partial(densify_kernel, odd),
        grid_spec=pltpu.PrefetchScalarGridSpec(
            num_scalar_prefetch=2,
            grid=(half,),
            in_specs=[
                pl.BlockSpec(
                    (1, 1, 1, slots, tile, tile),
                    lambda m, place, _: (
                        0, 0, jnp.bitwise_xor(place[0], 2 * chip_offset(m, half) + odd), 0, 0, 0
                    ),
                )
            ],
            out_specs=pl.BlockSpec(memory_space=pltpu.VMEM),
        ),
        out_shape=jax.ShapeDtypeStruct((depth, half * segment), jnp.bfloat16),
        name="densify_theirs" if odd else "densify_mine",
        compiler_params=params(),
        cost_estimate=CHEAP,
    )(place, codes, tile_values)


def multiply_kernel(offsets, first, rows, start, *refs):
    label_refs, matrix_ref, out_ref = refs[:-2], refs[-2], refs[-1]
    count, _, segment = out_ref.shape
    label_refs = [label_refs[offsets.index(k)] for k in range(len(offsets))]
    labels = jnp.concatenate([ref[first : first + rows, :] for ref in label_refs], axis=1)
    for i in range(0, count, 2):
        part = jnp.dot(
            labels,
            matrix_ref[:, (start + i) * segment : (start + i + 2) * segment],
            preferred_element_type=jnp.float32,
        )
        out_ref[i] = part[:, :segment].astype(out_ref.dtype)
        out_ref[i + 1] = part[:, segment:].astype(out_ref.dtype)


def multiply(sources, first, rows, matrix, dtype, name, start, count, weight):
    offsets, labels = sources
    segment = labels[0].shape[1]
    depth, width = matrix.shape
    return pl.pallas_call(
        functools.partial(multiply_kernel, tuple(offsets), first, rows, start),
        out_shape=jax.ShapeDtypeStruct((count, rows, segment), dtype),
        name=name,
        compiler_params=params(),
        cost_estimate=pl.CostEstimate(
            flops=2 * weight * depth * width * rows, bytes_accessed=1, transcendentals=0
        ),
    )(*labels, matrix)


def pair_kernel(start, mine_ref, theirs_ref, *out_refs):
    for i, out_ref in enumerate(out_refs):
        total = mine_ref[start + i] + theirs_ref[i].astype(jnp.float32)
        out_ref[...] = total.astype(out_ref.dtype)


def pair(mine, theirs, start=0):
    count, rows, segment = theirs.shape
    types = [jnp.bfloat16 if start + i else jnp.float32 for i in range(count)]
    return pl.pallas_call(
        functools.partial(pair_kernel, start),
        out_shape=[jax.ShapeDtypeStruct((rows, segment), dtype) for dtype in types],
        name="pair_sum",
        compiler_params=params(),
        cost_estimate=CHEAP,
    )(mine, theirs)


def halve_kernel(order, kept_ref, arrived_ref, stay_ref, send_ref):
    for i in range(kept_ref.shape[0]):
        total = kept_ref[order[i]] + arrived_ref[order[i]].astype(jnp.float32)
        if i % 2:
            send_ref[i // 2] = total.astype(send_ref.dtype)
        else:
            stay_ref[i // 2] = total


def halve(kept, arrived, order):
    count, rows, segment = kept.shape
    shape = (count // 2, rows, segment)
    return pl.pallas_call(
        functools.partial(halve_kernel, order),
        out_shape=[
            jax.ShapeDtypeStruct(shape, jnp.float32),
            jax.ShapeDtypeStruct(shape, jnp.bfloat16),
        ],
        name="halve_sum",
        compiler_params=params(),
        cost_estimate=CHEAP,
    )(kept, arrived)


def add_pieces(pieces):
    total = pieces[0][...].reshape(pieces[0].shape[-2:])
    for piece in pieces[1:]:
        total = total + piece[...].reshape(total.shape).astype(jnp.float32)
    return total


def middle_kernel(first_class, seed_ref, *refs):
    pieces, (grad_ref, next_ref) = refs[:-2], refs[-2:]
    grad = (ALPHA * add_pieces(pieces)).astype(jnp.bfloat16)
    grad_ref[...] = grad
    keep = keep_of(seed_ref[...][None, :], first_class, grad.shape[0])
    next_ref[...] = jnp.where(keep, grad.astype(jnp.float32), 0.0).astype(jnp.bfloat16)


def middle(seed_label, pieces, first_class):
    shape = jax.ShapeDtypeStruct(pieces[0].shape[-2:], jnp.bfloat16)
    return pl.pallas_call(
        functools.partial(middle_kernel, first_class),
        out_shape=[shape, shape],
        name="first_grad",
        compiler_params=params(),
        cost_estimate=pl.CostEstimate(
            flops=10**10 if first_class == 0 else 1, bytes_accessed=1, transcendentals=0
        ),
    )(seed_label, *pieces)


def turn_kernel(part_ref, out_ref):
    out_ref[...] = part_ref[...].astype(jnp.float32).T.astype(out_ref.dtype)


def turn(part):
    rows, segment = part.shape
    return pl.pallas_call(
        turn_kernel,
        out_shape=jax.ShapeDtypeStruct((segment, rows), part.dtype),
        name="turn_grad",
        compiler_params=params(),
        cost_estimate=pl.CostEstimate(flops=10**10, bytes_accessed=1, transcendentals=0),
    )(part)


def first_out_kernel(*refs):
    ready, last_ref, out_ref = refs[:-2], refs[-2], refs[-1]
    rows = last_ref.shape[0]
    for i, ref in enumerate(ready):
        out_ref[:, i * rows : (i + 1) * rows] = ref[...]
    turned = last_ref[...].astype(jnp.float32).T.astype(out_ref.dtype)
    out_ref[:, len(ready) * rows :] = turned


def first_out(ready, last):
    rows, segment = last.shape
    return pl.pallas_call(
        first_out_kernel,
        out_shape=jax.ShapeDtypeStruct((segment, (len(ready) + 1) * rows), jnp.bfloat16),
        name="first_grad_out",
        compiler_params=params(),
        cost_estimate=CHEAP,
    )(*ready, last)


def label_part(first, first_ref, second_ref, pieces):
    rows = second_ref.shape[0]
    kept = first_ref[first : first + rows, :].astype(jnp.float32)
    kept = kept + second_ref[...].astype(jnp.float32)
    return (ALPHA * add_pieces(pieces) + (1.0 - ALPHA) * kept).T.astype(jnp.bfloat16)


def label_kernel(first, first_ref, second_ref, *refs):
    refs[-1][...] = label_part(first, first_ref, second_ref, refs[:-1])


def label(first_in, second_in, pieces, first):
    rows, segment = second_in.shape
    return pl.pallas_call(
        functools.partial(label_kernel, first),
        out_shape=jax.ShapeDtypeStruct((segment, rows), jnp.bfloat16),
        name="label_grad",
        compiler_params=params(),
        cost_estimate=CHEAP,
    )(first_in, second_in, *pieces)


def last_label_kernel(first, count, first_ref, second_ref, *refs):
    ready, pieces, out_ref = refs[:count], refs[count:-1], refs[-1]
    rows = second_ref.shape[0]
    for i, ref in enumerate(ready):
        out_ref[:, i * rows : (i + 1) * rows] = ref[...]
    out_ref[:, first : first + rows] = label_part(first, first_ref, second_ref, pieces)


def last_label(first_in, second_in, pieces, first, ready):
    classes, segment = first_in.shape
    return pl.pallas_call(
        functools.partial(last_label_kernel, first, len(ready)),
        out_shape=jax.ShapeDtypeStruct((segment, classes), jnp.bfloat16),
        name="label_grad_out",
        compiler_params=params(),
        cost_estimate=CHEAP,
    )(first_in, second_in, *ready, *pieces)


def flip(array, axis, size, bits):
    return lax.ppermute(array, axis, [(i, i ^ bits) for i in range(size)])


def gather(labels, n_col, order, late=(), waits=()):
    held = after(labels, waits) if late else labels
    offsets = [k % n_col for k in order if k < n_col] + list(range(len(order) + 1, n_col))
    parts = [flip(held if k in late else labels, "col", n_col, k) for k in offsets]
    return [0] + offsets, [labels] + parts


def spread(parts, offsets, n_row):
    return parts[:1] + [
        flip(part, "row", n_row, 2 * j) for j, part in zip(offsets[1:], parts[1:])
    ]


def local(n_row, n_col, cotangent, seed_label, tile_values, tile_rows, tile_cols, tile_scale):
    segment, classes = cotangent.shape
    rows, depth = classes // 2, n_col * segment
    blocks, chips = segment // tile_values.shape[-1], n_row // 2
    offsets = [0, chips - 1, *range(1, chips - 1)]
    col_place = lax.axis_index("col").astype(jnp.int32)
    place = jnp.stack([lax.axis_index("row").astype(jnp.int32), col_place])
    first_in = prepare(cotangent, seed_label)
    codes = slot_codes(col_place, blocks, tile_rows[0, 0], tile_cols[0, 0], tile_scale[0, 0])
    to_theirs = densify(place, codes, tile_values, 1, depth, segment)
    to_mine = densify(place, after(codes, to_theirs), tile_values, 0, depth, segment)

    def for_theirs(labels, first, waits, splits=1, weight=0):
        parts, count = [], chips // splits
        for start in range(0, chips, count):
            labels = labels[0], after(labels[1], waits)
            waits = multiply(
                labels, first, rows, to_theirs, jnp.bfloat16, "multiply_theirs",
                start, count, weight,
            )
            parts.append(flip(waits, "row", n_row, 1))
        return waits, parts

    def for_mine(labels, first, waits, weight=0):
        labels = labels[0], after(labels[1], waits)
        return multiply(
            labels, first, rows, to_mine, jnp.float32, "multiply_mine", 0, chips, weight
        )

    def add_pairs(mine, swapped):
        parts = []
        for part in swapped:
            parts += pair(after(mine, parts), part, len(parts))
        return parts

    arrived = gather(first_in, n_col, (2, 1, 3))
    theirs, swapped_a = for_theirs(arrived, 0, to_mine, 2)
    mine = for_mine(arrived, 0, theirs)
    parts_a = add_pairs(mine, swapped_a)
    theirs, swapped_b = for_theirs(arrived, rows, parts_a)
    mine = for_mine(arrived, rows, theirs, 20)
    pieces_a = spread(parts_a, offsets, n_row)
    done = halve(mine, swapped_b[0], [offsets.index(j) for j in range(chips)])
    pieces_b = [done[0], flip(done[1], "row", n_row, 2)]

    grad_a, second_a = middle(seed_label, after(pieces_a, done), 0)
    done, step = [grad_a, second_a], 4
    while step < n_row:
        done = halve(*after(pieces_b, done), range(chips))
        pieces_b = [done[0], flip(done[1], "row", n_row, step)]
        step *= 2
    sources_a = gather(second_a, n_col, (3, 2, 1), (1,), done)
    turned_a = turn(after(grad_a, done))
    grad_b, second_b = middle(seed_label, after(pieces_b, turned_a), rows)

    theirs, swapped_a = for_theirs(sources_a, 0, [grad_b, second_b])
    mine = for_mine(sources_a, 0, theirs, 20)
    sources_b = gather(second_b, n_col, (3, 2, 1))
    parts_a = add_pairs(mine, swapped_a)
    theirs, swapped_b = for_theirs(sources_b, 0, parts_a, 1)
    mine = for_mine(sources_b, 0, theirs, 20)
    pieces_a = spread(parts_a, offsets, n_row)
    parts_b = add_pairs(mine, swapped_b)
    pieces_b = spread(parts_b, offsets, n_row)

    label_a = label(first_in, second_a, after(pieces_a, parts_b), 0)
    first_grad = first_out([turned_a], after(grad_b, label_a))
    pieces_b = after(pieces_b, first_grad)
    return first_grad, last_label(first_in, second_b, pieces_b, rows, [label_a])


def solution(mesh):
    return jax.shard_map(
        functools.partial(local, mesh.shape["row"], mesh.shape["col"]),
        mesh=mesh,
        in_specs=(
            P(("row", "col"), None),
            P(("row", "col")),
            P("row", "col", None, None, None, None),
            P("row", "col", None, None),
            P("row", "col", None, None),
            P("row", "col", None, None),
        ),
        out_specs=(P(("row", "col"), None), P(("row", "col"), None)),
        check_vma=False,
    )
```

```python
import functools

import jax
import jax.numpy as jnp
from jax import lax
from jax.experimental import pallas as pl
from jax.experimental.pallas import tpu as pltpu
from jax.sharding import PartitionSpec as P

ALPHA = 0.9
VMEM_LIMIT = 8 * 1024 * 1024
CHEAP = pl.CostEstimate(flops=1, bytes_accessed=1, transcendentals=0)


def params(limit=VMEM_LIMIT):
    return pltpu.CompilerParams(vmem_limit_bytes=limit)


def after(arrays, *others):
    return lax.optimization_barrier((arrays, others))[0]


def keep_of(seed_row, first_class, classes):
    ids = lax.broadcasted_iota(jnp.int32, (classes, seed_row.shape[1]), 0) + first_class
    return ids != seed_row


def prepare_kernel(cot_ref, seed_ref, out_ref, part_ref, cot, seed, semaphores):
    copies = [
        pltpu.make_async_copy(cot_ref, cot, semaphores.at[0]),
        pltpu.make_async_copy(seed_ref, seed, semaphores.at[1]),
    ]
    for copy in copies:
        copy.start()
    for copy in copies:
        copy.wait()
    part = cot[...].astype(jnp.float32).T
    keep = keep_of(seed[...][None, :], 0, part.shape[0])
    labels = jnp.where(keep, part, 0.0).astype(out_ref.dtype)
    out_ref[...] = labels
    part_ref[...] = labels[: part_ref.shape[0], :]


def prepare(cotangent, seed_label):
    segment, classes = cotangent.shape
    cotangent, seed_label = (
        pltpu.with_memory_space_constraint(array, pltpu.HBM) for array in (cotangent, seed_label)
    )
    return pl.pallas_call(
        prepare_kernel,
        in_specs=[pl.BlockSpec(memory_space=pltpu.HBM)] * 2,
        out_shape=[
            jax.ShapeDtypeStruct((count, segment), jnp.bfloat16)
            for count in (classes, classes // 2)
        ],
        scratch_shapes=[
            pltpu.VMEM(cotangent.shape, cotangent.dtype),
            pltpu.VMEM(seed_label.shape, seed_label.dtype),
            pltpu.SemaphoreType.DMA((2,)),
        ],
        name="prepare",
        cost_estimate=pl.CostEstimate(flops=10**10, bytes_accessed=1, transcendentals=0),
        compiler_params=params(),

    )(cotangent, seed_label)


def slot_codes(col_place, blocks, tile_rows, tile_cols, tile_scale):
    slots = tile_rows.shape[1]
    ids = jnp.arange(slots, dtype=jnp.int32)
    place = ((tile_rows // blocks) ^ col_place) * blocks + tile_rows % blocks
    codes = (((place << 4) | tile_cols) << 16) | (ids[None, :] << 8) | tile_scale
    position = jnp.sum((codes[:, None, :] < codes[:, :, None]).astype(jnp.int32), axis=-1)
    return jnp.sum(jnp.where(position[:, :, None] == ids, codes[:, :, None], 0), axis=1)


def chip_offset(position, chips):
    return jnp.where(position == 0, 0, (position + chips - 3) % (chips - 1) + 1)


def target_of(step, steps, row_place):
    half = steps // 2
    odd = jnp.where(step < half, 1, 0)
    return jnp.bitwise_xor(row_place, 2 * chip_offset(step % half, half) + odd)


def densify_kernel(place_ref, codes_ref, tiles_ref, out_ref, held_ref, semaphores):
    targets, slots, tile, _ = held_ref.shape
    segment = out_ref.shape[1] // targets

    def copy_of(step):
        target = target_of(step, targets, place_ref[0])
        return pltpu.make_async_copy(
            tiles_ref.at[0, 0, target], held_ref.at[step], semaphores.at[step]
        )

    for step in range(targets):
        copy_of(step).start()
    out_ref[...] = jnp.zeros_like(out_ref)

    def build(step, carry):
        target = target_of(step, targets, place_ref[0])
        base = step * segment
        copy_of(step).wait()

        def add(position, carry):
            total, before = carry
            code = codes_ref[target, position]
            block, slot, scale = code >> 16, (code >> 8) & 255, code & 255
            term = held_ref[step, slot].astype(jnp.float32) * scale.astype(jnp.float32)
            total = total * (block == before).astype(jnp.float32) + term
            row, col = (block >> 4) * tile, base + (block & 15) * tile
            out_ref[
                pl.ds(pl.multiple_of(row, tile), tile), pl.ds(pl.multiple_of(col, tile), tile)
            ] = total.astype(out_ref.dtype)
            return total, block

        start = (jnp.zeros((tile, tile), jnp.float32), jnp.int32(-1))
        lax.fori_loop(0, slots, add, start, unroll=4)
        return carry

    lax.fori_loop(0, targets, build, 0)


def densify(place, codes, tile_values, depth, segment):
    _, _, targets, slots, tile, _ = tile_values.shape
    size = 2 * depth * targets * segment + 2 * tile_values.size
    return pl.pallas_call(
        densify_kernel,
        in_specs=[pl.BlockSpec(memory_space=pltpu.SMEM)] * 2
        + [pl.BlockSpec(memory_space=pltpu.HBM)],
        out_specs=pl.BlockSpec(memory_space=pltpu.VMEM),
        out_shape=jax.ShapeDtypeStruct((depth, targets * segment), jnp.bfloat16),
        scratch_shapes=[
            pltpu.VMEM((targets, slots, tile, tile), tile_values.dtype),
            pltpu.SemaphoreType.DMA((targets,)),
        ],
        name="densify",
        compiler_params=params(size + VMEM_LIMIT // 2),
    )(place, codes, pltpu.with_memory_space_constraint(tile_values, pltpu.HBM))


def multiply_kernel(offsets, firsts, rows, start, *refs):
    count = len(offsets)
    label_refs, matrix_ref, out_refs = refs[:count], refs[count], refs[count + 1 :]
    parts = {
        k: ref[first : first + rows, :] for k, first, ref in zip(offsets, firsts, label_refs)
    }
    labels = jnp.concatenate([parts[k] for k in range(count)], axis=1)
    for out_ref in out_refs:
        targets, _, segment = out_ref.shape
        for i in range(0, targets, 2):
            part = jnp.dot(
                labels,
                matrix_ref[:, (start + i) * segment : (start + i + 2) * segment],
                preferred_element_type=jnp.float32,
            )
            out_ref[i] = part[:, :segment].astype(out_ref.dtype)
            out_ref[i + 1] = part[:, segment:].astype(out_ref.dtype)
        start += targets


def multiply(sources, rows, matrix, dtype, name, start, count, weight, pieces=1):
    offsets, firsts, labels = sources
    segment = labels[0].shape[1]
    depth, width = matrix.shape
    shape = jax.ShapeDtypeStruct((count // pieces, rows, segment), dtype)
    return pl.pallas_call(
        functools.partial(multiply_kernel, tuple(offsets), tuple(firsts), rows, start),
        out_shape=[shape] * pieces,
        name=name,
        compiler_params=params(2 * depth * width + VMEM_LIMIT),
        cost_estimate=pl.CostEstimate(
            flops=2 * weight * depth * width * rows, bytes_accessed=1, transcendentals=0
        ),
    )(*labels, matrix)


def pair_kernel(start, mine_ref, theirs_ref, *out_refs):
    for i, out_ref in enumerate(out_refs):
        total = mine_ref[start + i] + theirs_ref[i].astype(jnp.float32)
        out_ref[...] = total.astype(out_ref.dtype)


def pair(mine, theirs, start=0):
    count, rows, segment = theirs.shape
    types = [jnp.bfloat16 if start + i else jnp.float32 for i in range(count)]
    return pl.pallas_call(
        functools.partial(pair_kernel, start),
        out_shape=[jax.ShapeDtypeStruct((rows, segment), dtype) for dtype in types],
        name="pair_sum",
        compiler_params=params(),
        cost_estimate=CHEAP,
    )(mine, theirs)


def halve_kernel(order, kept_ref, arrived_ref, stay_ref, send_ref):
    for i in range(kept_ref.shape[0]):
        total = kept_ref[order[i]] + arrived_ref[order[i]].astype(jnp.float32)
        if i % 2:
            send_ref[i // 2] = total.astype(send_ref.dtype)
        else:
            stay_ref[i // 2] = total


def halve(kept, arrived, order):
    count, rows, segment = kept.shape
    shape = (count // 2, rows, segment)
    return pl.pallas_call(
        functools.partial(halve_kernel, order),
        out_shape=[
            jax.ShapeDtypeStruct(shape, jnp.float32),
            jax.ShapeDtypeStruct(shape, jnp.bfloat16),
        ],
        name="halve_sum",
        compiler_params=params(),
        cost_estimate=CHEAP,
    )(kept, arrived)


def add_pieces(pieces):
    total = pieces[0][...].reshape(pieces[0].shape[-2:])
    for piece in pieces[1:]:
        total = total + piece[...].reshape(total.shape).astype(jnp.float32)
    return total


def middle_kernel(first_class, seed_ref, *refs):
    pieces, (grad_ref, next_ref) = refs[:-2], refs[-2:]
    grad = (ALPHA * add_pieces(pieces)).astype(jnp.bfloat16)
    grad_ref[...] = grad
    keep = keep_of(seed_ref[...][None, :], first_class, grad.shape[0])
    next_ref[...] = jnp.where(keep, grad.astype(jnp.float32), 0.0).astype(jnp.bfloat16)


def middle(seed_label, pieces, first_class):
    shape = jax.ShapeDtypeStruct(pieces[0].shape[-2:], jnp.bfloat16)
    return pl.pallas_call(
        functools.partial(middle_kernel, first_class),
        out_shape=[shape, shape],
        name="first_grad",
        compiler_params=params(),
        cost_estimate=pl.CostEstimate(
            flops=10**10 if first_class == 0 else 1, bytes_accessed=1, transcendentals=0
        ),
    )(seed_label, *pieces)


def turn_kernel(part_ref, out_ref):
    out_ref[...] = part_ref[...].astype(jnp.float32).T.astype(out_ref.dtype)


def turn(part):
    rows, segment = part.shape
    return pl.pallas_call(
        turn_kernel,
        out_shape=jax.ShapeDtypeStruct((segment, rows), part.dtype),
        name="turn_grad",
        compiler_params=params(),
        cost_estimate=pl.CostEstimate(flops=10**10, bytes_accessed=1, transcendentals=0),
    )(part)


def first_out_kernel(*refs):
    ready, last_ref, out_ref = refs[:-2], refs[-2], refs[-1]
    rows = last_ref.shape[0]
    for i, ref in enumerate(ready):
        out_ref[:, i * rows : (i + 1) * rows] = ref[...]
    turned = last_ref[...].astype(jnp.float32).T.astype(out_ref.dtype)
    out_ref[:, len(ready) * rows :] = turned


def first_out(ready, last):
    rows, segment = last.shape
    return pl.pallas_call(
        first_out_kernel,
        out_shape=jax.ShapeDtypeStruct((segment, (len(ready) + 1) * rows), jnp.bfloat16),
        name="first_grad_out",
        compiler_params=params(),
        cost_estimate=CHEAP,
    )(*ready, last)


def label_part(first, first_ref, second_ref, pieces):
    rows = second_ref.shape[0]
    kept = first_ref[first : first + rows, :].astype(jnp.float32)
    kept = kept + second_ref[...].astype(jnp.float32)
    return (ALPHA * add_pieces(pieces) + (1.0 - ALPHA) * kept).T.astype(jnp.bfloat16)


def label_kernel(first, first_ref, second_ref, *refs):
    refs[-1][...] = label_part(first, first_ref, second_ref, refs[:-1])


def label(first_in, second_in, pieces, first):
    rows, segment = second_in.shape
    return pl.pallas_call(
        functools.partial(label_kernel, first),
        out_shape=jax.ShapeDtypeStruct((segment, rows), jnp.bfloat16),
        name="label_grad",
        compiler_params=params(),
        cost_estimate=CHEAP,
    )(first_in, second_in, *pieces)


def last_label_kernel(first, count, first_ref, second_ref, *refs):
    ready, pieces, out_ref = refs[:count], refs[count:-1], refs[-1]
    rows = second_ref.shape[0]
    for i, ref in enumerate(ready):
        out_ref[:, i * rows : (i + 1) * rows] = ref[...]
    out_ref[:, first : first + rows] = label_part(first, first_ref, second_ref, pieces)


def last_label(first_in, second_in, pieces, first, ready):
    classes, segment = first_in.shape
    return pl.pallas_call(
        functools.partial(last_label_kernel, first, len(ready)),
        out_shape=jax.ShapeDtypeStruct((segment, classes), jnp.bfloat16),
        name="label_grad_out",
        compiler_params=params(),
        cost_estimate=CHEAP,
    )(first_in, second_in, *ready, *pieces)


def flip(array, axis, size, bits):
    return lax.ppermute(array, axis, [(i, i ^ bits) for i in range(size)])


def stack_kernel(own_ref, arrived_ref, out_ref):
    rows = out_ref.shape[0] // 2
    out_ref[:rows, :] = own_ref[rows:, :]
    out_ref[rows:, :] = arrived_ref[rows:, :]


def stack(own, arrived):
    return pl.pallas_call(
        stack_kernel,
        out_shape=jax.ShapeDtypeStruct(own.shape, own.dtype),
        name="stack_labels",
        compiler_params=params(),
        cost_estimate=CHEAP,
    )(own, arrived)


def gather(labels, n_col, order, late=(), waits=()):
    held = after(labels, waits) if late else labels
    offsets = [k for k in order if k < n_col] + list(range(len(order) + 1, n_col))
    parts = [flip(held if k in late else labels, "col", n_col, k) for k in offsets]
    return [0] + offsets, [0] * n_col, [labels] + parts


def gather_both(labels, part, n_col, waits):
    rows, half = part.shape[0], n_col // 2
    across = flip(labels, "col", n_col, half)
    others = [k for k in range(1, n_col) if k != half]
    parts = [flip(part, "col", n_col, k) for k in others]
    first = [0, half] + others, [0] * n_col, [labels, across] + parts
    both, across = after((labels, across), waits)
    both = stack(both, across)
    sources = [0, half], [rows, rows], [labels, across]
    for k in range(1, half):
        arrived = flip(both, "col", n_col, k)
        for values, more in zip(sources, ([k, k ^ half], [0, rows], [arrived, arrived])):
            values.extend(more)
    return first, sources, both


def spread(parts, offsets, n_row):
    return parts[:1] + [
        flip(part, "row", n_row, 2 * j) for j, part in zip(offsets[1:], parts[1:])
    ]


def local(n_row, n_col, cotangent, seed_label, tile_values, tile_rows, tile_cols, tile_scale):
    segment, classes = cotangent.shape
    rows, depth = classes // 2, n_col * segment
    blocks, chips = segment // tile_values.shape[-1], n_row // 2
    offsets = [0, chips - 1, *range(1, chips - 1)]
    col_place = lax.axis_index("col").astype(jnp.int32)
    place = jnp.stack([lax.axis_index("row").astype(jnp.int32), col_place])
    first_in, first_a = prepare(cotangent, seed_label)
    codes = slot_codes(col_place, blocks, tile_rows[0, 0], tile_cols[0, 0], tile_scale[0, 0])
    matrix = densify(place, codes, tile_values, depth, segment)
    sources_a, sources_b, both = gather_both(first_in, first_a, n_col, matrix)

    def for_theirs(labels, waits, pieces=1):
        labels = *labels[:2], after(labels[2], waits)
        parts = multiply(
            labels, rows, matrix, jnp.bfloat16, "multiply_theirs", 0, chips, 0, pieces
        )
        return parts, [flip(part, "row", n_row, 1) for part in parts]

    def for_mine(labels, waits, weight=0):
        labels = *labels[:2], after(labels[2], waits)
        return multiply(
            labels, rows, matrix, jnp.float32, "multiply_mine", chips, chips, weight
        )[0]

    def add_pairs(mine, swapped):
        parts = []
        for part in swapped:
            parts += pair(after(mine, parts), part, len(parts))
        return parts

    theirs, swapped_a = for_theirs(sources_a, both, 2)
    mine = for_mine(sources_a, theirs, 20)
    parts_a = add_pairs(mine, swapped_a)
    theirs, swapped_b = for_theirs(sources_b, parts_a)
    mine = for_mine(sources_b, theirs, 20)
    pieces_a = spread(parts_a, offsets, n_row)
    done = halve(mine, swapped_b[0], [offsets.index(j) for j in range(chips)])
    pieces_b = [done[0], flip(done[1], "row", n_row, 2)]

    grad_a, second_a = middle(seed_label, after(pieces_a, done), 0)
    done, step = [grad_a, second_a], 4
    while step < n_row:
        done = halve(*after(pieces_b, done), range(chips))
        pieces_b = [done[0], flip(done[1], "row", n_row, step)]
        step *= 2
    sources_a = gather(second_a, n_col, (3, 2, 1), (1,), done)
    turned_a = turn(after(grad_a, done))
    grad_b, second_b = middle(seed_label, after(pieces_b, turned_a), rows)

    theirs, swapped_a = for_theirs(sources_a, [grad_b, second_b])
    mine = for_mine(sources_a, theirs, 20)
    sources_b = gather(second_b, n_col, (3, 2, 1))
    parts_a = add_pairs(mine, swapped_a)
    theirs, swapped_b = for_theirs(sources_b, parts_a)
    mine = for_mine(sources_b, theirs, 20)
    pieces_a = spread(parts_a, offsets, n_row)
    parts_b = add_pairs(mine, swapped_b)
    pieces_b = spread(parts_b, offsets, n_row)

    label_a = label(first_in, second_a, after(pieces_a, parts_b), 0)
    first_grad = first_out([turned_a], after(grad_b, label_a))
    pieces_b = after(pieces_b, first_grad)
    return first_grad, last_label(first_in, second_b, pieces_b, rows, [label_a])


def solution(mesh):
    return jax.shard_map(
        functools.partial(local, mesh.shape["row"], mesh.shape["col"]),
        mesh=mesh,
        in_specs=(
            P(("row", "col"), None),
            P(("row", "col")),
            P("row", "col", None, None, None, None),
            P("row", "col", None, None),
            P("row", "col", None, None),
            P("row", "col", None, None),
        ),
        out_specs=(P(("row", "col"), None), P(("row", "col"), None)),
        check_vma=False,
    )
```

```python
import functools

import jax
import jax.numpy as jnp
from jax import lax
from jax.experimental import pallas as pl
from jax.experimental.pallas import tpu as pltpu
from jax.sharding import PartitionSpec as P

ALPHA = 0.9
VMEM_LIMIT = 8 * 1024 * 1024
CHEAP = pl.CostEstimate(flops=1, bytes_accessed=1, transcendentals=0)


def params(limit=VMEM_LIMIT):
    return pltpu.CompilerParams(vmem_limit_bytes=limit)


def after(arrays, *others):
    return lax.optimization_barrier((arrays, others))[0]


def keep_of(seed_row, first_class, classes):
    ids = lax.broadcasted_iota(jnp.int32, (classes, seed_row.shape[1]), 0) + first_class
    return ids != seed_row


def prepare_kernel(cot_ref, seed_ref, out_ref, first_ref, last_ref, cot, seed, semaphores):
    copies = [
        pltpu.make_async_copy(cot_ref, cot, semaphores.at[0]),
        pltpu.make_async_copy(seed_ref, seed, semaphores.at[1]),
    ]
    for copy in copies:
        copy.start()
    for copy in copies:
        copy.wait()
    part = cot[...].astype(jnp.float32).T
    keep = keep_of(seed[...][None, :], 0, part.shape[0])
    labels = jnp.where(keep, part, 0.0).astype(out_ref.dtype)
    out_ref[...] = labels
    rows = first_ref.shape[0]
    first_ref[...] = labels[:rows, :]
    last_ref[...] = labels[rows:, :]


def prepare(cotangent, seed_label):
    segment, classes = cotangent.shape
    cotangent, seed_label = (
        pltpu.with_memory_space_constraint(array, pltpu.HBM) for array in (cotangent, seed_label)
    )
    return pl.pallas_call(
        prepare_kernel,
        in_specs=[pl.BlockSpec(memory_space=pltpu.HBM)] * 2,
        out_shape=[
            jax.ShapeDtypeStruct((count, segment), jnp.bfloat16)
            for count in (classes, classes // 2, classes // 2)
        ],
        scratch_shapes=[
            pltpu.VMEM(cotangent.shape, cotangent.dtype),
            pltpu.VMEM(seed_label.shape, seed_label.dtype),
            pltpu.SemaphoreType.DMA((2,)),
        ],
        name="prepare",
        cost_estimate=pl.CostEstimate(flops=10**10, bytes_accessed=1, transcendentals=0),
        compiler_params=params(),

    )(cotangent, seed_label)


def slot_codes(col_place, blocks, tile_rows, tile_cols, tile_scale):
    slots = tile_rows.shape[1]
    ids = jnp.arange(slots, dtype=jnp.int32)
    place = ((tile_rows // blocks) ^ col_place) * blocks + tile_rows % blocks
    codes = (((place << 4) | tile_cols) << 16) | (ids[None, :] << 8) | tile_scale
    position = jnp.sum((codes[:, None, :] < codes[:, :, None]).astype(jnp.int32), axis=-1)
    return jnp.sum(jnp.where(position[:, :, None] == ids, codes[:, :, None], 0), axis=1)


def chip_offset(position, chips):
    return jnp.where(position == 0, 0, (position + chips - 3) % (chips - 1) + 1)


def target_of(step, steps, row_place):
    half = steps // 2
    odd = jnp.where(step < half, 1, 0)
    return jnp.bitwise_xor(row_place, 2 * chip_offset(step % half, half) + odd)


def densify_kernel(place_ref, codes_ref, tiles_ref, out_ref, held_ref, semaphores):
    targets, slots, tile, _ = held_ref.shape
    segment = out_ref.shape[1] // targets

    def copy_of(step):
        target = target_of(step, targets, place_ref[0])
        return pltpu.make_async_copy(
            tiles_ref.at[0, 0, target], held_ref.at[step], semaphores.at[step]
        )

    for step in range(targets):
        copy_of(step).start()
    out_ref[...] = jnp.zeros_like(out_ref)

    def build(step, carry):
        target = target_of(step, targets, place_ref[0])
        base = step * segment
        copy_of(step).wait()

        def add(position, carry):
            total, before = carry
            code = codes_ref[target, position]
            block, slot, scale = code >> 16, (code >> 8) & 255, code & 255
            term = held_ref[step, slot].astype(jnp.float32) * scale.astype(jnp.float32)
            total = total * (block == before).astype(jnp.float32) + term
            row, col = (block >> 4) * tile, base + (block & 15) * tile
            out_ref[
                pl.ds(pl.multiple_of(row, tile), tile), pl.ds(pl.multiple_of(col, tile), tile)
            ] = total.astype(out_ref.dtype)
            return total, block

        start = (jnp.zeros((tile, tile), jnp.float32), jnp.int32(-1))
        lax.fori_loop(0, slots, add, start, unroll=4)
        return carry

    lax.fori_loop(0, targets, build, 0)


def densify(place, codes, tile_values, depth, segment):
    _, _, targets, slots, tile, _ = tile_values.shape
    size = 2 * depth * targets * segment + 2 * tile_values.size
    return pl.pallas_call(
        densify_kernel,
        in_specs=[pl.BlockSpec(memory_space=pltpu.SMEM)] * 2
        + [pl.BlockSpec(memory_space=pltpu.HBM)],
        out_specs=pl.BlockSpec(memory_space=pltpu.VMEM),
        out_shape=jax.ShapeDtypeStruct((depth, targets * segment), jnp.bfloat16),
        scratch_shapes=[
            pltpu.VMEM((targets, slots, tile, tile), tile_values.dtype),
            pltpu.SemaphoreType.DMA((targets,)),
        ],
        name="densify",
        compiler_params=params(size + VMEM_LIMIT // 2),
    )(place, codes, pltpu.with_memory_space_constraint(tile_values, pltpu.HBM))


def multiply_kernel(offsets, firsts, rows, start, *refs):
    count = len(offsets)
    label_refs, matrix_ref, out_refs = refs[:count], refs[count], refs[count + 1 :]
    parts = {
        k: ref[first : first + rows, :] for k, first, ref in zip(offsets, firsts, label_refs)
    }
    labels = jnp.concatenate([parts[k] for k in range(count)], axis=1)
    for out_ref in out_refs:
        targets, _, segment = out_ref.shape
        for i in range(0, targets, 2):
            part = jnp.dot(
                labels,
                matrix_ref[:, (start + i) * segment : (start + i + 2) * segment],
                preferred_element_type=jnp.float32,
            )
            out_ref[i] = part[:, :segment].astype(out_ref.dtype)
            out_ref[i + 1] = part[:, segment:].astype(out_ref.dtype)
        start += targets


def multiply(sources, rows, matrix, dtype, name, start, count, weight, pieces=1):
    offsets, firsts, labels = sources
    segment = labels[0].shape[1]
    depth, width = matrix.shape
    shape = jax.ShapeDtypeStruct((count // pieces, rows, segment), dtype)
    return pl.pallas_call(
        functools.partial(multiply_kernel, tuple(offsets), tuple(firsts), rows, start),
        out_shape=[shape] * pieces,
        name=name,
        compiler_params=params(2 * depth * width + VMEM_LIMIT),
        cost_estimate=pl.CostEstimate(
            flops=2 * weight * depth * width * rows, bytes_accessed=1, transcendentals=0
        ),
    )(*labels, matrix)


def pair_kernel(start, mine_ref, theirs_ref, *out_refs):
    for i, out_ref in enumerate(out_refs):
        total = mine_ref[start + i] + theirs_ref[i].astype(jnp.float32)
        out_ref[...] = total.astype(out_ref.dtype)


def pair(mine, theirs, start=0):
    count, rows, segment = theirs.shape
    types = [jnp.bfloat16 if start + i else jnp.float32 for i in range(count)]
    return pl.pallas_call(
        functools.partial(pair_kernel, start),
        out_shape=[jax.ShapeDtypeStruct((rows, segment), dtype) for dtype in types],
        name="pair_sum",
        compiler_params=params(),
        cost_estimate=CHEAP,
    )(mine, theirs)


def halve_kernel(order, kept_ref, arrived_ref, stay_ref, send_ref):
    for i in range(kept_ref.shape[0]):
        total = kept_ref[order[i]] + arrived_ref[order[i]].astype(jnp.float32)
        if i % 2:
            send_ref[i // 2] = total.astype(send_ref.dtype)
        else:
            stay_ref[i // 2] = total


def halve(kept, arrived, order):
    count, rows, segment = kept.shape
    shape = (count // 2, rows, segment)
    return pl.pallas_call(
        functools.partial(halve_kernel, order),
        out_shape=[
            jax.ShapeDtypeStruct(shape, jnp.float32),
            jax.ShapeDtypeStruct(shape, jnp.bfloat16),
        ],
        name="halve_sum",
        compiler_params=params(),
        cost_estimate=CHEAP,
    )(kept, arrived)


def add_pieces(pieces):
    total = pieces[0][...].reshape(pieces[0].shape[-2:])
    for piece in pieces[1:]:
        total = total + piece[...].reshape(total.shape).astype(jnp.float32)
    return total


def middle_kernel(first_class, seed_ref, *refs):
    pieces, (grad_ref, next_ref) = refs[:-2], refs[-2:]
    grad = (ALPHA * add_pieces(pieces)).astype(jnp.bfloat16)
    grad_ref[...] = grad
    keep = keep_of(seed_ref[...][None, :], first_class, grad.shape[0])
    next_ref[...] = jnp.where(keep, grad.astype(jnp.float32), 0.0).astype(jnp.bfloat16)


def middle(seed_label, pieces, first_class):
    shape = jax.ShapeDtypeStruct(pieces[0].shape[-2:], jnp.bfloat16)
    return pl.pallas_call(
        functools.partial(middle_kernel, first_class),
        out_shape=[shape, shape],
        name="first_grad",
        compiler_params=params(),
        cost_estimate=pl.CostEstimate(
            flops=10**10 if first_class == 0 else 1, bytes_accessed=1, transcendentals=0
        ),
    )(seed_label, *pieces)


def turn_kernel(part_ref, out_ref):
    out_ref[...] = part_ref[...].astype(jnp.float32).T.astype(out_ref.dtype)


def turn(part):
    rows, segment = part.shape
    return pl.pallas_call(
        turn_kernel,
        out_shape=jax.ShapeDtypeStruct((segment, rows), part.dtype),
        name="turn_grad",
        compiler_params=params(),
        cost_estimate=pl.CostEstimate(flops=10**10, bytes_accessed=1, transcendentals=0),
    )(part)


def first_out_kernel(*refs):
    ready, last_ref, out_ref = refs[:-2], refs[-2], refs[-1]
    rows = last_ref.shape[0]
    for i, ref in enumerate(ready):
        out_ref[:, i * rows : (i + 1) * rows] = ref[...]
    turned = last_ref[...].astype(jnp.float32).T.astype(out_ref.dtype)
    out_ref[:, len(ready) * rows :] = turned


def first_out(ready, last):
    rows, segment = last.shape
    return pl.pallas_call(
        first_out_kernel,
        out_shape=jax.ShapeDtypeStruct((segment, (len(ready) + 1) * rows), jnp.bfloat16),
        name="first_grad_out",
        compiler_params=params(),
        cost_estimate=CHEAP,
    )(*ready, last)


def label_part(first, first_ref, second_ref, pieces):
    rows = second_ref.shape[0]
    kept = first_ref[first : first + rows, :].astype(jnp.float32)
    kept = kept + second_ref[...].astype(jnp.float32)
    return (ALPHA * add_pieces(pieces) + (1.0 - ALPHA) * kept).T.astype(jnp.bfloat16)


def label_kernel(first, first_ref, second_ref, *refs):
    refs[-1][...] = label_part(first, first_ref, second_ref, refs[:-1])


def label(first_in, second_in, pieces, first):
    rows, segment = second_in.shape
    return pl.pallas_call(
        functools.partial(label_kernel, first),
        out_shape=jax.ShapeDtypeStruct((segment, rows), jnp.bfloat16),
        name="label_grad",
        compiler_params=params(),
        cost_estimate=CHEAP,
    )(first_in, second_in, *pieces)


def last_label_kernel(first, count, first_ref, second_ref, *refs):
    ready, pieces, out_ref = refs[:count], refs[count:-1], refs[-1]
    rows = second_ref.shape[0]
    for i, ref in enumerate(ready):
        out_ref[:, i * rows : (i + 1) * rows] = ref[...]
    out_ref[:, first : first + rows] = label_part(first, first_ref, second_ref, pieces)


def last_label(first_in, second_in, pieces, first, ready):
    classes, segment = first_in.shape
    return pl.pallas_call(
        functools.partial(last_label_kernel, first, len(ready)),
        out_shape=jax.ShapeDtypeStruct((segment, classes), jnp.bfloat16),
        name="label_grad_out",
        compiler_params=params(),
        cost_estimate=CHEAP,
    )(first_in, second_in, *ready, *pieces)


def flip(array, axis, size, bits):
    return lax.ppermute(array, axis, [(i, i ^ bits) for i in range(size)])


def stack_kernel(own_ref, arrived_ref, out_ref):
    rows = own_ref.shape[0]
    out_ref[:rows, :] = own_ref[...]
    out_ref[rows:, :] = arrived_ref[...]


def stack(own, arrived):
    rows, segment = own.shape
    return pl.pallas_call(
        stack_kernel,
        out_shape=jax.ShapeDtypeStruct((2 * rows, segment), own.dtype),
        name="stack_labels",
        compiler_params=params(),
        cost_estimate=CHEAP,
    )(own, arrived)


def gather(labels, n_col, order, late=(), waits=()):
    held = after(labels, waits) if late else labels
    offsets = [k for k in order if k < n_col] + list(range(len(order) + 1, n_col))
    parts = [flip(held if k in late else labels, "col", n_col, k) for k in offsets]
    return [0] + offsets, [0] * n_col, [labels] + parts


def gather_both(first, last, n_col, waits):
    rows, half = first.shape[0], n_col // 2
    others = [half] + [k for k in range(1, n_col) if k != half]
    parts = [flip(first, "col", n_col, k) for k in others]
    across = flip(last, "col", n_col, half)
    sources_first = [0] + others, [0] * n_col, [first] + parts
    both = stack(*after((last, across), waits))
    sources = [0, half], [0, 0], [last, across]
    for k in range(1, half):
        arrived = flip(both, "col", n_col, k)
        for values, more in zip(sources, ([k, k ^ half], [0, rows], [arrived, arrived])):
            values.extend(more)
    return sources_first, sources, both


def spread(parts, offsets, n_row):
    return parts[:1] + [
        flip(part, "row", n_row, 2 * j) for j, part in zip(offsets[1:], parts[1:])
    ]


def local(n_row, n_col, cotangent, seed_label, tile_values, tile_rows, tile_cols, tile_scale):
    segment, classes = cotangent.shape
    rows, depth = classes // 2, n_col * segment
    blocks, chips = segment // tile_values.shape[-1], n_row // 2
    offsets = [0, chips - 1, *range(1, chips - 1)]
    col_place = lax.axis_index("col").astype(jnp.int32)
    place = jnp.stack([lax.axis_index("row").astype(jnp.int32), col_place])
    first_in, first_a, first_b = prepare(cotangent, seed_label)
    codes = slot_codes(col_place, blocks, tile_rows[0, 0], tile_cols[0, 0], tile_scale[0, 0])
    matrix = densify(place, codes, tile_values, depth, segment)
    sources_a, sources_b, both = gather_both(first_a, first_b, n_col, matrix)

    def for_theirs(labels, waits, pieces=1):
        labels = *labels[:2], after(labels[2], waits)
        parts = multiply(
            labels, rows, matrix, jnp.bfloat16, "multiply_theirs", 0, chips, 0, pieces
        )
        return parts, [flip(part, "row", n_row, 1) for part in parts]

    def for_mine(labels, waits, weight=0):
        labels = *labels[:2], after(labels[2], waits)
        return multiply(
            labels, rows, matrix, jnp.float32, "multiply_mine", chips, chips, weight
        )[0]

    def add_pairs(mine, swapped):
        parts = []
        for part in swapped:
            parts += pair(after(mine, parts), part, len(parts))
        return parts

    theirs, swapped_a = for_theirs(sources_a, both, 2)
    mine = for_mine(sources_a, theirs, 20)
    parts_a = add_pairs(mine, swapped_a)
    theirs, swapped_b = for_theirs(sources_b, parts_a)
    mine = for_mine(sources_b, theirs, 20)
    pieces_a = spread(parts_a, offsets, n_row)
    done = halve(mine, swapped_b[0], [offsets.index(j) for j in range(chips)])
    pieces_b = [done[0], flip(done[1], "row", n_row, 2)]

    grad_a, second_a = middle(seed_label, after(pieces_a, done), 0)
    done, step = [grad_a, second_a], 4
    while step < n_row:
        done = halve(*after(pieces_b, done), range(chips))
        pieces_b = [done[0], flip(done[1], "row", n_row, step)]
        step *= 2
    sources_a = gather(second_a, n_col, (3, 2, 1), (1,), done)
    turned_a = turn(after(grad_a, done))
    grad_b, second_b = middle(seed_label, after(pieces_b, turned_a), rows)

    theirs, swapped_a = for_theirs(sources_a, [grad_b, second_b], 2)
    mine = for_mine(sources_a, theirs, 20)
    sources_b = gather(second_b, n_col, (3, 2, 1))
    parts_a = add_pairs(mine, swapped_a)
    theirs, swapped_b = for_theirs(sources_b, parts_a, 2)
    mine = for_mine(sources_b, theirs, 20)
    pieces_a = spread(parts_a, offsets, n_row)
    parts_b = add_pairs(mine, swapped_b)
    pieces_b = spread(parts_b, offsets, n_row)

    label_a = label(first_in, second_a, after(pieces_a, parts_b), 0)
    first_grad = first_out([turned_a], after(grad_b, label_a))
    pieces_b = after(pieces_b, first_grad)
    return first_grad, last_label(first_in, second_b, pieces_b, rows, [label_a])


def solution(mesh):
    return jax.shard_map(
        functools.partial(local, mesh.shape["row"], mesh.shape["col"]),
        mesh=mesh,
        in_specs=(
            P(("row", "col"), None),
            P(("row", "col")),
            P("row", "col", None, None, None, None),
            P("row", "col", None, None),
            P("row", "col", None, None),
            P("row", "col", None, None),
        ),
        out_specs=(P(("row", "col"), None), P(("row", "col"), None)),
        check_vma=False,
    )
```

```python
import functools

import jax
import jax.numpy as jnp
from jax import lax
from jax.experimental import pallas as pl
from jax.experimental.pallas import tpu as pltpu
from jax.sharding import PartitionSpec as P

ALPHA = 0.9
VMEM_LIMIT = 8 * 1024 * 1024
CHEAP = pl.CostEstimate(flops=1, bytes_accessed=1, transcendentals=0)


def params(limit=VMEM_LIMIT):
    return pltpu.CompilerParams(vmem_limit_bytes=limit)


def after(arrays, *others):
    return lax.optimization_barrier((arrays, others))[0]


def keep_of(seed_row, first_class, classes):
    ids = lax.broadcasted_iota(jnp.int32, (classes, seed_row.shape[1]), 0) + first_class
    return ids != seed_row


def prepare_kernel(cot_ref, seed_ref, out_ref, first_ref, last_ref, cot, seed, semaphores):
    copies = [
        pltpu.make_async_copy(cot_ref, cot, semaphores.at[0]),
        pltpu.make_async_copy(seed_ref, seed, semaphores.at[1]),
    ]
    for copy in copies:
        copy.start()
    for copy in copies:
        copy.wait()
    part = cot[...].astype(jnp.float32).T
    keep = keep_of(seed[...][None, :], 0, part.shape[0])
    labels = jnp.where(keep, part, 0.0).astype(out_ref.dtype)
    out_ref[...] = labels
    rows = first_ref.shape[0]
    first_ref[...] = labels[:rows, :]
    last_ref[...] = labels[rows:, :]


def prepare(cotangent, seed_label):
    segment, classes = cotangent.shape
    cotangent, seed_label = (
        pltpu.with_memory_space_constraint(array, pltpu.HBM) for array in (cotangent, seed_label)
    )
    return pl.pallas_call(
        prepare_kernel,
        in_specs=[pl.BlockSpec(memory_space=pltpu.HBM)] * 2,
        out_shape=[
            jax.ShapeDtypeStruct((count, segment), jnp.bfloat16)
            for count in (classes, classes // 2, classes // 2)
        ],
        scratch_shapes=[
            pltpu.VMEM(cotangent.shape, cotangent.dtype),
            pltpu.VMEM(seed_label.shape, seed_label.dtype),
            pltpu.SemaphoreType.DMA((2,)),
        ],
        name="prepare",
        cost_estimate=pl.CostEstimate(flops=10**10, bytes_accessed=1, transcendentals=0),
        compiler_params=params(),

    )(cotangent, seed_label)


def slot_codes(col_place, blocks, tile_rows, tile_cols, tile_scale):
    slots = tile_rows.shape[1]
    ids = jnp.arange(slots, dtype=jnp.int32)
    place = ((tile_rows // blocks) ^ col_place) * blocks + tile_rows % blocks
    codes = (((place << 4) | tile_cols) << 16) | (ids[None, :] << 8) | tile_scale
    position = jnp.sum((codes[:, None, :] < codes[:, :, None]).astype(jnp.int32), axis=-1)
    return jnp.sum(jnp.where(position[:, :, None] == ids, codes[:, :, None], 0), axis=1)


def chip_offset(position, chips):
    return jnp.where(position == 0, 0, (position + chips - 3) % (chips - 1) + 1)


def target_of(step, steps, row_place):
    half = steps // 2
    odd = jnp.where(step < half, 1, 0)
    return jnp.bitwise_xor(row_place, 2 * chip_offset(step % half, half) + odd)


def densify_kernel(place_ref, codes_ref, tiles_ref, out_ref, held_ref, semaphores):
    targets, slots, tile, _ = held_ref.shape
    segment = out_ref.shape[1] // targets

    def copy_of(step):
        target = target_of(step, targets, place_ref[0])
        return pltpu.make_async_copy(
            tiles_ref.at[0, 0, target], held_ref.at[step], semaphores.at[step]
        )

    for step in range(targets):
        copy_of(step).start()
    out_ref[...] = jnp.zeros_like(out_ref)

    def build(step, carry):
        target = target_of(step, targets, place_ref[0])
        base = step * segment
        copy_of(step).wait()

        def add(position, carry):
            total, before = carry
            code = codes_ref[target, position]
            block, slot, scale = code >> 16, (code >> 8) & 255, code & 255
            term = held_ref[step, slot].astype(jnp.float32) * scale.astype(jnp.float32)
            total = total * (block == before).astype(jnp.float32) + term
            row, col = (block >> 4) * tile, base + (block & 15) * tile
            out_ref[
                pl.ds(pl.multiple_of(row, tile), tile), pl.ds(pl.multiple_of(col, tile), tile)
            ] = total.astype(out_ref.dtype)
            return total, block

        start = (jnp.zeros((tile, tile), jnp.float32), jnp.int32(-1))
        lax.fori_loop(0, slots, add, start, unroll=4)
        return carry

    lax.fori_loop(0, targets, build, 0)


def densify(place, codes, tile_values, depth, segment):
    _, _, targets, slots, tile, _ = tile_values.shape
    size = 2 * depth * targets * segment + 2 * tile_values.size
    return pl.pallas_call(
        densify_kernel,
        in_specs=[pl.BlockSpec(memory_space=pltpu.SMEM)] * 2
        + [pl.BlockSpec(memory_space=pltpu.HBM)],
        out_specs=pl.BlockSpec(memory_space=pltpu.VMEM),
        out_shape=jax.ShapeDtypeStruct((depth, targets * segment), jnp.bfloat16),
        scratch_shapes=[
            pltpu.VMEM((targets, slots, tile, tile), tile_values.dtype),
            pltpu.SemaphoreType.DMA((targets,)),
        ],
        name="densify",
        compiler_params=params(size + VMEM_LIMIT // 2),
    )(place, codes, pltpu.with_memory_space_constraint(tile_values, pltpu.HBM))


def multiply_kernel(offsets, firsts, rows, start, *refs):
    count = len(offsets)
    label_refs, matrix_ref, out_refs = refs[:count], refs[count], refs[count + 1 :]
    parts = {
        k: ref[first : first + rows, :] for k, first, ref in zip(offsets, firsts, label_refs)
    }
    labels = jnp.concatenate([parts[k] for k in range(count)], axis=1)
    for out_ref in out_refs:
        targets, _, segment = out_ref.shape
        for i in range(0, targets, 2):
            part = jnp.dot(
                labels,
                matrix_ref[:, (start + i) * segment : (start + i + 2) * segment],
                preferred_element_type=jnp.float32,
            )
            out_ref[i] = part[:, :segment].astype(out_ref.dtype)
            out_ref[i + 1] = part[:, segment:].astype(out_ref.dtype)
        start += targets


def multiply(sources, rows, matrix, dtype, name, start, count, weight, pieces=1):
    offsets, firsts, labels = sources
    segment = labels[0].shape[1]
    depth, width = matrix.shape
    shape = jax.ShapeDtypeStruct((count // pieces, rows, segment), dtype)
    return pl.pallas_call(
        functools.partial(multiply_kernel, tuple(offsets), tuple(firsts), rows, start),
        out_shape=[shape] * pieces,
        name=name,
        compiler_params=params(2 * depth * width + VMEM_LIMIT),
        cost_estimate=pl.CostEstimate(
            flops=2 * weight * depth * width * rows, bytes_accessed=1, transcendentals=0
        ),
    )(*labels, matrix)


def pair_kernel(start, mine_ref, theirs_ref, *out_refs):
    for i, out_ref in enumerate(out_refs):
        total = mine_ref[start + i] + theirs_ref[i].astype(jnp.float32)
        out_ref[...] = total.astype(out_ref.dtype)


def pair(mine, theirs, start=0):
    count, rows, segment = theirs.shape
    types = [jnp.bfloat16 if start + i else jnp.float32 for i in range(count)]
    return pl.pallas_call(
        functools.partial(pair_kernel, start),
        out_shape=[jax.ShapeDtypeStruct((rows, segment), dtype) for dtype in types],
        name="pair_sum",
        compiler_params=params(),
        cost_estimate=CHEAP,
    )(mine, theirs)


def halve_kernel(order, kept_ref, *refs):
    arrived_refs, (stay_ref, send_ref) = refs[:-2], refs[-2:]
    arrived = [ref.at[i] for ref in arrived_refs for i in range(ref.shape[0])]
    for i in range(kept_ref.shape[0]):
        total = kept_ref[order[i]] + arrived[order[i]][...].astype(jnp.float32)
        if i % 2:
            send_ref[i // 2] = total.astype(send_ref.dtype)
        else:
            stay_ref[i // 2] = total


def halve(kept, arrived, order):
    count, rows, segment = kept.shape
    shape = (count // 2, rows, segment)
    return pl.pallas_call(
        functools.partial(halve_kernel, order),
        out_shape=[
            jax.ShapeDtypeStruct(shape, jnp.float32),
            jax.ShapeDtypeStruct(shape, jnp.bfloat16),
        ],
        name="halve_sum",
        compiler_params=params(),
        cost_estimate=CHEAP,
    )(kept, *arrived)


def add_pieces(pieces):
    total = pieces[0][...].reshape(pieces[0].shape[-2:])
    for piece in pieces[1:]:
        total = total + piece[...].reshape(total.shape).astype(jnp.float32)
    return total


def middle_kernel(first_class, seed_ref, *refs):
    pieces, (grad_ref, next_ref) = refs[:-2], refs[-2:]
    grad = (ALPHA * add_pieces(pieces)).astype(jnp.bfloat16)
    grad_ref[...] = grad
    keep = keep_of(seed_ref[...][None, :], first_class, grad.shape[0])
    next_ref[...] = jnp.where(keep, grad.astype(jnp.float32), 0.0).astype(jnp.bfloat16)


def middle(seed_label, pieces, first_class):
    shape = jax.ShapeDtypeStruct(pieces[0].shape[-2:], jnp.bfloat16)
    return pl.pallas_call(
        functools.partial(middle_kernel, first_class),
        out_shape=[shape, shape],
        name="first_grad",
        compiler_params=params(),
        cost_estimate=pl.CostEstimate(
            flops=10**10 if first_class == 0 else 1, bytes_accessed=1, transcendentals=0
        ),
    )(seed_label, *pieces)


def turn_kernel(part_ref, out_ref):
    out_ref[...] = part_ref[...].astype(jnp.float32).T.astype(out_ref.dtype)


def turn(part):
    rows, segment = part.shape
    return pl.pallas_call(
        turn_kernel,
        out_shape=jax.ShapeDtypeStruct((segment, rows), part.dtype),
        name="turn_grad",
        compiler_params=params(),
        cost_estimate=pl.CostEstimate(flops=10**10, bytes_accessed=1, transcendentals=0),
    )(part)


def first_out_kernel(*refs):
    ready, last_ref, out_ref = refs[:-2], refs[-2], refs[-1]
    rows = last_ref.shape[0]
    for i, ref in enumerate(ready):
        out_ref[:, i * rows : (i + 1) * rows] = ref[...]
    turned = last_ref[...].astype(jnp.float32).T.astype(out_ref.dtype)
    out_ref[:, len(ready) * rows :] = turned


def first_out(ready, last):
    rows, segment = last.shape
    return pl.pallas_call(
        first_out_kernel,
        out_shape=jax.ShapeDtypeStruct((segment, (len(ready) + 1) * rows), jnp.bfloat16),
        name="first_grad_out",
        compiler_params=params(),
        cost_estimate=CHEAP,
    )(*ready, last)


def label_part(first, first_ref, second_ref, pieces):
    rows = second_ref.shape[0]
    kept = first_ref[first : first + rows, :].astype(jnp.float32)
    kept = kept + second_ref[...].astype(jnp.float32)
    return (ALPHA * add_pieces(pieces) + (1.0 - ALPHA) * kept).T.astype(jnp.bfloat16)


def label_kernel(first, first_ref, second_ref, *refs):
    refs[-1][...] = label_part(first, first_ref, second_ref, refs[:-1])


def label(first_in, second_in, pieces, first):
    rows, segment = second_in.shape
    return pl.pallas_call(
        functools.partial(label_kernel, first),
        out_shape=jax.ShapeDtypeStruct((segment, rows), jnp.bfloat16),
        name="label_grad",
        compiler_params=params(),
        cost_estimate=CHEAP,
    )(first_in, second_in, *pieces)


def last_label_kernel(first, count, first_ref, second_ref, *refs):
    ready, pieces, out_ref = refs[:count], refs[count:-1], refs[-1]
    rows = second_ref.shape[0]
    for i, ref in enumerate(ready):
        out_ref[:, i * rows : (i + 1) * rows] = ref[...]
    out_ref[:, first : first + rows] = label_part(first, first_ref, second_ref, pieces)


def last_label(first_in, second_in, pieces, first, ready):
    classes, segment = first_in.shape
    return pl.pallas_call(
        functools.partial(last_label_kernel, first, len(ready)),
        out_shape=jax.ShapeDtypeStruct((segment, classes), jnp.bfloat16),
        name="label_grad_out",
        compiler_params=params(),
        cost_estimate=CHEAP,
    )(first_in, second_in, *ready, *pieces)


def flip(array, axis, size, bits):
    return lax.ppermute(array, axis, [(i, i ^ bits) for i in range(size)])


def stack_kernel(own_ref, arrived_ref, out_ref):
    rows = own_ref.shape[0]
    out_ref[:rows, :] = own_ref[...]
    out_ref[rows:, :] = arrived_ref[...]


def stack(own, arrived):
    rows, segment = own.shape
    return pl.pallas_call(
        stack_kernel,
        out_shape=jax.ShapeDtypeStruct((2 * rows, segment), own.dtype),
        name="stack_labels",
        compiler_params=params(),
        cost_estimate=CHEAP,
    )(own, arrived)


def gather(labels, n_col, order, late=(), waits=()):
    held = after(labels, waits) if late else labels
    offsets = [k for k in order if k < n_col] + list(range(len(order) + 1, n_col))
    parts = [flip(held if k in late else labels, "col", n_col, k) for k in offsets]
    return [0] + offsets, [0] * n_col, [labels] + parts


def gather_both(first, last, n_col, waits):
    rows, half = first.shape[0], n_col // 2
    others = [half] + [k for k in range(1, n_col) if k != half]
    parts = [flip(first, "col", n_col, k) for k in others]
    across = flip(last, "col", n_col, half)
    sources_first = [0] + others, [0] * n_col, [first] + parts
    both = stack(*after((last, across), waits))
    sources = [0, half], [0, 0], [last, across]
    for k in range(1, half):
        arrived = flip(both, "col", n_col, k)
        for values, more in zip(sources, ([k, k ^ half], [0, rows], [arrived, arrived])):
            values.extend(more)
    return sources_first, sources, both


def spread(parts, offsets, n_row):
    return parts[:1] + [
        flip(part, "row", n_row, 2 * j) for j, part in zip(offsets[1:], parts[1:])
    ]


def local(n_row, n_col, cotangent, seed_label, tile_values, tile_rows, tile_cols, tile_scale):
    segment, classes = cotangent.shape
    rows, depth = classes // 2, n_col * segment
    blocks, chips = segment // tile_values.shape[-1], n_row // 2
    offsets = [0, chips - 1, *range(1, chips - 1)]
    col_place = lax.axis_index("col").astype(jnp.int32)
    place = jnp.stack([lax.axis_index("row").astype(jnp.int32), col_place])
    first_in, first_a, first_b = prepare(cotangent, seed_label)
    codes = slot_codes(col_place, blocks, tile_rows[0, 0], tile_cols[0, 0], tile_scale[0, 0])
    matrix = densify(place, codes, tile_values, depth, segment)
    sources_a, sources_b, both = gather_both(first_a, first_b, n_col, matrix)

    def for_theirs(labels, waits, pieces=1):
        labels = *labels[:2], after(labels[2], waits)
        parts = multiply(
            labels, rows, matrix, jnp.bfloat16, "multiply_theirs", 0, chips, 0, pieces
        )
        return parts, [flip(part, "row", n_row, 1) for part in parts]

    def for_mine(labels, waits, weight=0):
        labels = *labels[:2], after(labels[2], waits)
        return multiply(
            labels, rows, matrix, jnp.float32, "multiply_mine", chips, chips, weight
        )[0]

    def add_pairs(mine, swapped):
        parts = []
        for part in swapped:
            parts += pair(after(mine, parts), part, len(parts))
        return parts

    theirs, swapped_a = for_theirs(sources_a, both, 2)
    mine = for_mine(sources_a, theirs, 20)
    parts_a = add_pairs(mine, swapped_a)
    theirs, swapped_b = for_theirs(sources_b, parts_a, 2)
    mine = for_mine(sources_b, theirs, 20)
    pieces_a = spread(parts_a, offsets, n_row)
    done = halve(mine, swapped_b, [offsets.index(j) for j in range(chips)])
    pieces_b = [done[0], flip(done[1], "row", n_row, 2)]

    grad_a, second_a = middle(seed_label, after(pieces_a, done), 0)
    done, step = [grad_a, second_a], 4
    while step < n_row:
        kept, arrived = after(pieces_b, done)
        done = halve(kept, [arrived], range(chips))
        pieces_b = [done[0], flip(done[1], "row", n_row, step)]
        step *= 2
    sources_a = gather(second_a, n_col, (3, 2, 1), (1,), done)
    turned_a = turn(after(grad_a, done))
    grad_b, second_b = middle(seed_label, after(pieces_b, turned_a), rows)

    theirs, swapped_a = for_theirs(sources_a, [grad_b, second_b], 2)
    mine = for_mine(sources_a, theirs, 20)
    sources_b = gather(second_b, n_col, (3, 2, 1))
    parts_a = add_pairs(mine, swapped_a)
    theirs, swapped_b = for_theirs(sources_b, parts_a, 2)
    mine = for_mine(sources_b, theirs, 20)
    pieces_a = spread(parts_a, offsets, n_row)
    parts_b = add_pairs(mine, swapped_b)
    pieces_b = spread(parts_b, offsets, n_row)

    label_a = label(first_in, second_a, after(pieces_a, parts_b), 0)
    first_grad = first_out([turned_a], after(grad_b, label_a))
    pieces_b = after(pieces_b, first_grad)
    return first_grad, last_label(first_in, second_b, pieces_b, rows, [label_a])


def solution(mesh):
    return jax.shard_map(
        functools.partial(local, mesh.shape["row"], mesh.shape["col"]),
        mesh=mesh,
        in_specs=(
            P(("row", "col"), None),
            P(("row", "col")),
            P("row", "col", None, None, None, None),
            P("row", "col", None, None),
            P("row", "col", None, None),
            P("row", "col", None, None),
        ),
        out_specs=(P(("row", "col"), None), P(("row", "col"), None)),
        check_vma=False,
    )
```
